256 devices in a mesh: dp: 32 (over z, x), tensor: 8 (over y, core).
Axes of the slice: x: 4, y: 4, z: 8, core: 2. Of those that a mesh axis runs over, the one named last changes fastest.
Arguments:
- queries: bfloat16 [512, 128, 4096], P(('dp', 'tensor')), may hold values from -5 to 5, as said below
- keys: bfloat16 [512, 128, 1024], P(('dp', 'tensor')), may hold values from -5 to 5, as said below
- values: bfloat16 [512, 128, 1024], P(('dp', 'tensor')), may hold values from -6 to 6
- out_grad: bfloat16 [512, 128, 4096], P(('dp', 'tensor')), may hold values from -24 to 24
- out_weight: bfloat16 [4096, 4096], P('tensor'), may hold values from -0.09375 to 0.09375
- lengths: int32 [512], P(('dp', 'tensor')), may hold values from 4 to 124, as said below
- dest_group: int32 [512], P(('dp', 'tensor')), may hold values from 0 to 31, as said below
- dest_offset: int32 [512], P(('dp', 'tensor')), may hold values from 0 to 124, as said below
Outputs:
- query_grad: bfloat16 [32768, 4096], P(('dp', 'tensor'))
- key_grad: bfloat16 [32768, 1024], P(('dp', 'tensor'))
- value_grad: bfloat16 [32768, 1024], P(('dp', 'tensor'))
- weight_grad: float32 [4096, 4096], P('tensor', 'dp')
The draws below stay inside these ranges and needn't reach their ends.
Inputs may be any that keep to these rules, and one draw needn't show every extreme that they name: queries of order one. keys of order one. Slot r holds a rollout row of lengths[r] tokens at its start; the rest of the slot is padding. `dest_group`: a row's destination group is its own index along dp or the one 32 // 2 away; it keeps its index along tensor. Every device receives exactly 2 rows, whose lengths sum to 128. `dest_offset`: the rows packed into one device don't intersect and fill its 128 positions.
All inputs are finite; a program needn't handle non-finite values.
Results may differ from the reference program's by a relative error of at most 0.027.
Values may be sent and summed in bfloat16 or wider, within the bound.
A program may use at most 128 MiB of HBM per device.

```python
import jax
import jax.numpy as jnp
from jax import lax

D = 4096
HEADS = 32
KV_HEADS = 8
HEAD_DIM = 128
TOK_DEV = 128
SLOTS = 2
ROWS = 512
DEST_TOKENS = 32768
N_DP = 32
N_TENSOR = 8


def rollout_plan(key):
    key = jax.random.fold_in(key, 202)
    half = N_DP // 2
    key_len, key_order = jax.random.split(key)
    first = jax.random.randint(key_len, (2, half, N_TENSOR), 4, TOK_DEV - 3)
    first = first.at[0, 0, 0].set(TOK_DEV - 4)
    row_len = jnp.stack([first[0], TOK_DEV - first[0], first[1], TOK_DEV - first[1]], -1)
    zeros_int = jnp.zeros_like(first[0])
    row_off = jnp.stack([zeros_int, first[0], zeros_int, first[1]], -1)
    lower = jnp.broadcast_to(jnp.arange(half, dtype=jnp.int32)[:, None], (half, N_TENSOR))
    row_dest = jnp.stack([lower, lower, lower + half, lower + half], -1)
    scores = jax.random.randint(key_order, (half, N_TENSOR, 4), 0, 1024) * 4 + jnp.arange(4, dtype=jnp.int32)
    order = jnp.argsort(scores, axis=-1)

    def arrange(table):
        dealt = jnp.take_along_axis(table, order, axis=-1)
        whole = jnp.concatenate([dealt[:, :, 0:2], dealt[:, :, 2:4]], axis=0)
        return whole.reshape(ROWS).astype(jnp.int32)
    return (arrange(row_len), arrange(row_dest), arrange(row_off))


def draw_queries(key, part):
    key = jax.random.fold_in(key, 3)
    shape = (ROWS, TOK_DEV, HEADS * HEAD_DIM)
    base = jax.random.truncated_normal(key, -5.0, 5.0, shape, jnp.float32)
    return base.astype(jnp.bfloat16)


def draw_keys(key, part):
    key = jax.random.fold_in(key, 5)
    shape = (ROWS, TOK_DEV, KV_HEADS * HEAD_DIM)
    base = jax.random.truncated_normal(key, -5.0, 5.0, shape, jnp.float32)
    return base.astype(jnp.bfloat16)


def draw_lengths(key, part):
    plan = rollout_plan(key)
    return plan[0]


def draw_dest_group(key, part):
    plan = rollout_plan(key)
    return plan[1]


def draw_dest_offset(key, part):
    plan = rollout_plan(key)
    return plan[2]


def with_spikes(values, rng, source, target, blocks, factor):
    owner, partner = [(jnp.arange(values.shape[dim]) // (values.shape[dim] // blocks)).reshape([-1 if axis == dim else 1 for axis in range(values.ndim)]) for dim in (source, target)]
    chosen = jax.random.permutation(rng, blocks)[partner]
    strong = (owner == chosen) | (owner == (partner + blocks // 2) % blocks)
    return jnp.where(strong, factor * values, values)


def level_of(key, dims, pieces, low, top_value):
    gain, own = 1.0, jax.random.fold_in(key, 6)
    for position, blocks in pieces:
        draws = jnp.exp(jax.random.uniform(jax.random.fold_in(own, position), (blocks,), jnp.float32, low / len(pieces), top_value / len(pieces)))
        gain = gain * jnp.repeat(draws, dims[position] // blocks).reshape([-1 if axis == position else 1 for axis in range(len(dims))])
    return gain


def scatter_about(stream_key, dims, scale, reach, shards=(), held_as=jnp.bfloat16):
    level = level_of(stream_key, dims, shards, -0.22, 0.18) if shards else 1.0
    entries = jax.random.normal(stream_key, dims, jnp.float32) * scale * level
    return jnp.minimum(jnp.maximum(entries, -reach), reach).astype(held_as)


def noise_with(key, extent, scale, reach, cuts, heavy, kind=jnp.bfloat16):
    drawn = scale * jax.random.normal(key, extent, jnp.float32)
    if cuts:
        drawn = drawn * level_of(key, extent, cuts, -0.22, 0.18)
    return jnp.clip(with_spikes(drawn, jax.random.fold_in(key, 3), *heavy), -reach, reach).astype(kind)


def setup_inputs(seed: int = 0) -> dict:
    streams_of = jax.random.split(jax.random.key(seed), 9)
    return {
        "queries": draw_queries(jax.random.fold_in(streams_of[8], 71), 0),
        "keys": draw_keys(jax.random.fold_in(streams_of[8], 71), 0),
        "values": scatter_about(streams_of[2], (ROWS, TOK_DEV, KV_HEADS * HEAD_DIM), 1.0, 6.0, ((0, 256),)),
        "out_grad": noise_with(streams_of[3], (ROWS, TOK_DEV, D), 1.0, 24.0, ((0, 256),), (0, 2, 256, 6.0)),
        "out_weight": scatter_about(streams_of[4], (D, D), D ** -0.5, 0.09375, ((0, 8),)),
        "lengths": draw_lengths(jax.random.fold_in(streams_of[8], 71), 0),
        "dest_group": draw_dest_group(jax.random.fold_in(streams_of[8], 71), 0),
        "dest_offset": draw_dest_offset(jax.random.fold_in(streams_of[8], 71), 0),
    }


def reference(queries, keys, values, out_grad, out_weight, lengths, dest_group, dest_offset):
    scale = float(HEAD_DIM) ** -0.5
    group_size = HEADS // KV_HEADS
    posit = jnp.arange(TOK_DEV, dtype=jnp.int32)

    def row_probs(query_row, key_row, length):
        query_f = query_row.astype(jnp.float32).reshape(TOK_DEV, KV_HEADS, group_size, HEAD_DIM)
        key_f = key_row.astype(jnp.float32).reshape(TOK_DEV, KV_HEADS, HEAD_DIM)
        scores = jnp.einsum("ickd,jcd->ckij", query_f, key_f) * scale
        valid = posit < length
        allowed = valid[:, None] & valid[None, :] & (posit[None, :] <= posit[:, None])
        top = jnp.max(jnp.where(allowed, scores, -1e30), axis=-1, keepdims=True)
        expo = jnp.where(allowed, jnp.exp(scores - top), 0.0)
        total = jnp.where(valid[:, None], jnp.sum(expo, axis=-1, keepdims=True), 1.0)
        return expo / total, query_f, key_f

    def forward_row(packet):
        query_row, key_row, value_row, length = packet
        probs, query_f, key_f = row_probs(query_row, key_row, length)
        probs_b = lax.optimization_barrier(probs.astype(jnp.bfloat16)).astype(jnp.float32)
        value_f = value_row.astype(jnp.float32).reshape(TOK_DEV, KV_HEADS, HEAD_DIM)
        attended = jnp.einsum("ckij,jcd->ickd", probs_b, value_f)
        return attended.reshape(TOK_DEV, D).astype(jnp.bfloat16)

    attended = lax.map(forward_row, (queries, keys, values, lengths))
    flat_att = attended.reshape(ROWS * TOK_DEV, D)
    flat_grad = out_grad.reshape(ROWS * TOK_DEV, D)
    weight_grad = lax.dot_general(flat_att, flat_grad, (((0,), (0,)), ((), ())), preferred_element_type=jnp.float32)
    att_grad = lax.dot_general(flat_grad, out_weight, (((1,), (1,)), ((), ())), preferred_element_type=jnp.float32)
    att_grad = att_grad.astype(jnp.bfloat16).reshape(ROWS, TOK_DEV, D)

    def backward_row(packet):
        query_row, key_row, value_row, length, att_row, grad_row = packet
        probs, query_f, key_f = row_probs(query_row, key_row, length)
        probs_b = lax.optimization_barrier(probs.astype(jnp.bfloat16)).astype(jnp.float32)
        value_f = value_row.astype(jnp.float32).reshape(TOK_DEV, KV_HEADS, HEAD_DIM)
        grad_f = grad_row.astype(jnp.float32).reshape(TOK_DEV, KV_HEADS, group_size, HEAD_DIM)
        att_f = att_row.astype(jnp.float32).reshape(TOK_DEV, KV_HEADS, group_size, HEAD_DIM)
        delta = jnp.sum(grad_f * att_f, axis=-1).transpose(1, 2, 0)
        prob_grad = jnp.einsum("ickd,jcd->ckij", grad_f, value_f)
        score_grad = probs * (prob_grad - delta[..., None])
        score_b = lax.optimization_barrier(score_grad.astype(jnp.bfloat16)).astype(jnp.float32)
        query_grad = (jnp.einsum("ckij,jcd->ickd", score_b, key_f) * scale).reshape(TOK_DEV, D)
        key_grad = (jnp.einsum("ckij,ickd->jcd", score_b, query_f) * scale).reshape(TOK_DEV, KV_HEADS * HEAD_DIM)
        value_grad = jnp.einsum("ckij,ickd->jcd", probs_b, grad_f).reshape(TOK_DEV, KV_HEADS * HEAD_DIM)
        return (query_grad.astype(jnp.bfloat16), key_grad.astype(jnp.bfloat16), value_grad.astype(jnp.bfloat16))

    row_query, row_key, row_value = lax.map(backward_row, (queries, keys, values, lengths, attended, att_grad))
    slot_tensor = (jnp.arange(ROWS, dtype=jnp.int32) // SLOTS) % N_TENSOR
    start = (dest_group * N_TENSOR + slot_tensor) * TOK_DEV + dest_offset
    target = start[:, None] + posit[None, :]
    target = jnp.where(posit[None, :] < lengths[:, None], target, DEST_TOKENS).reshape(-1)

    def packed(rows_grad):
        width = rows_grad.shape[-1]
        empty = jnp.zeros((DEST_TOKENS, width), jnp.bfloat16)
        return empty.at[target].set(rows_grad.reshape(-1, width), mode="drop")

    return (packed(row_query), packed(row_key), packed(row_value), weight_grad)
```

```python
import functools

import jax
import jax.numpy as jnp
from jax import lax
from jax.experimental import pallas as pl
from jax.experimental.pallas import tpu as pltpu
from jax.sharding import PartitionSpec as P

MESH = pl.DeviceIdType.MESH
BF = jnp.bfloat16
F32 = jnp.float32
HD = 128
T = 128
X = 4
Z = 8
NT = 8
KV = 8
GROUP = 4
NN = (((1,), (0,)), ((), ()))
NTD = (((1,), (1,)), ((), ()))
TN = (((0,), (0,)), ((), ()))


def dot(a, b, dims=NN):
    return lax.dot_general(a, b, dims, preferred_element_type=F32)


def tile(index, size=128):
    start = index * size
    if not isinstance(index, int):
        start = pl.multiple_of(start, size)
    return pl.ds(start, size)


def kernel(
    q_hbm, k_hbm, v_hbm, g_hbm, w_hbm, len_ref, grp_ref, off_ref,
    qg_ref, kg_ref, vg_ref, wg_ref,
    xin, wv, pack, mask, lab_s, lab_r,
    send, keep, got, gall,
    ag_s, ag_r, at_s, at_r, probs, outs, dk, dv,
    xs, xr, zs, zr,
    in_sem, zsend, zrecv, lsem, ysend, yrecv, csend, crecv,
    agsend, agrecv, atsend, atrecv, xsend, xrecv, rsend, rrecv,
):
    dp = lax.axis_index("dp")
    t = lax.axis_index("tensor")
    z = dp // X
    x = dp % X

    def at_z(d):
        return (lax.rem(z + d, Z) * X + x, t)

    def at_x(d):
        return (z * X + lax.rem(x + d, X), t)

    def at_t(d):
        return (dp, lax.rem(t + d, NT))

    partner = at_z(Z // 2)
    sibling_t = t + 1 - 2 * lax.rem(t, 2)
    sibling = (dp, sibling_t)

    def rcopy(src, dst, ssem, rsem, device):
        return pltpu.make_async_remote_copy(
            src_ref=src, dst_ref=dst, send_sem=ssem, recv_sem=rsem,
            device_id=device, device_id_type=MESH,
        )

    barrier = pltpu.get_barrier_semaphore()
    peers = [at_z(d) for d in range(1, Z)] + [at_x(d) for d in range(1, X)]
    peers = peers + [at_t(d) for d in range(1, NT)]
    for peer in peers:
        pl.semaphore_signal(barrier, inc=1, device_id=peer, device_id_type=MESH)

    loads = []
    for hbm, start, width in ((g_hbm, 0, 4096), (k_hbm, 4096, 1024), (v_hbm, 5120, 1024), (q_hbm, 6144, 4096)):
        for slot in range(2):
            loads.append(
                pltpu.make_async_copy(
                    hbm.at[slot],
                    xin.at[slot * T : (slot + 1) * T, start : start + width],
                    in_sem.at[len(loads)],
                )
            )
    loads.append(pltpu.make_async_copy(w_hbm, wv, in_sem.at[len(loads)]))
    for load in loads:
        load.start()

    rows = lax.broadcasted_iota(jnp.int32, (T, T), 0)
    cols = lax.broadcasted_iota(jnp.int32, (T, T), 1)
    moved_off = jnp.int32(0)
    kept_off = jnp.int32(0)
    for slot in range(2):
        length = len_ref[slot]
        offset = off_ref[slot]
        moving = jnp.where(grp_ref[slot] != dp, 1, 0)
        hit = jnp.where((cols < length) & (rows == cols + offset), 1.0, 0.0)
        went = moving.astype(F32)
        pack[0:T, slot * T : (slot + 1) * T] = (hit * went).astype(BF)
        pack[T : 2 * T, slot * T : (slot + 1) * T] = (hit * (1.0 - went)).astype(BF)
        moved_off = moved_off + moving * offset
        kept_off = kept_off + (1 - moving) * offset
    lab_s[...] = jnp.zeros((8, 128), jnp.int32) + moved_off

    def zcopy(i):
        return rcopy(send.at[i], got.at[i], zsend.at[i], zrecv.at[i], partner)

    label_copy = rcopy(lab_s, lab_r, lsem.at[0], lsem.at[1], partner)

    def packed(start):
        return dot(pack[...], xin[:, pl.ds(pl.multiple_of(start, 512), 512)])

    loads[0].wait()
    loads[1].wait()
    own_rows = tile(t)
    for i in range(4):
        for half in range(2):
            both = packed(i * 1024 + half * 512).astype(BF)
            send[i, :, half * 512 : (half + 1) * 512] = both[0:T]
            gall[own_rows, i * 1024 + half * 512 : i * 1024 + (half + 1) * 512] = both[T:]
        if i == 0:
            pl.semaphore_wait(barrier, len(peers))
            label_copy.start()
            zcopy(0).start()
        if i == 1:
            zcopy(1).start()
    for load in loads[2:8]:
        load.wait()
    for i in range(2):
        for half in range(2):
            both = packed(4096 + i * 1024 + half * 512).astype(BF)
            send[4 + i, :, half * 512 : (half + 1) * 512] = both[0:T]
            keep[i, :, half * 512 : (half + 1) * 512] = both[T:]

    def pack_q(c, carry):
        both = packed(6144 + c * 512).astype(BF)
        for j in range(GROUP):
            part = both[:, j * HD : (j + 1) * HD]
            send[6 + j, :, tile(c)] = part[0:T]
            keep[2 + j, :, tile(c)] = part[T:]
        return carry

    lax.fori_loop(0, KV, pack_q, 0)

    def block(i, row_t):
        return gall.at[tile(row_t), i * 1024 : (i + 1) * 1024]

    def ycopy(i, n, row_t):
        return rcopy(block(i, row_t), block(i, row_t), ysend.at[i, n], yrecv.at[i, n], at_t(2 * (n + 1)))

    def ccopy(i, n, row_t):
        return rcopy(block(i, row_t), block(i, row_t), csend.at[i, n], crecv.at[i, n], sibling)

    def from_t(n):
        return lax.rem(t + NT - 2 * (n + 1), NT)

    def sib_from_t(n):
        return lax.rem(sibling_t + NT - 2 * (n + 1), NT)

    def forward(i):
        for n in (0, 2, 1):
            ycopy(i, n, from_t(n)).wait_recv()
            ccopy(i, n, from_t(n)).start()

    for i in range(4):
        zcopy(i).wait_recv()
        zcopy(i + 2).start()
        lanes = slice(i * 1024, (i + 1) * 1024)
        gall[own_rows, lanes] = gall[own_rows, lanes] + got[i]
        for n in (1, 0, 2):
            ycopy(i, n, t).start()
        ccopy(i, 3, t).start()
        if i > 0:
            forward(i - 1)
    forward(3)
    loads[8].wait()
    for i in range(4):
        for n in range(3):
            ccopy(i, n, sib_from_t(n)).wait_recv()
        ccopy(i, 3, sibling_t).wait_recv()

    def ag_copy(d):
        peer = lax.rem(t + d, NT)
        return rcopy(
            ag_s.at[tile(peer), :], ag_r.at[:, tile(t, 512)],
            agsend.at[d - 1], agrecv.at[d - 1], at_t(d),
        )

    def ag_got(d):
        source = lax.rem(t + NT - d, NT)
        return rcopy(
            ag_s.at[tile(source), :], ag_r.at[:, tile(source, 512)],
            agsend.at[d - 1], agrecv.at[d - 1], at_t(d),
        )

    def ag_block(peer):
        return dot(gall[tile(peer), :], wv[...], NTD).astype(BF)

    def ag_step(d, carry):
        peer = lax.rem(t + d, NT)
        ag_s[tile(peer), :] = ag_block(peer)
        ag_copy(d).start()
        return carry

    lax.fori_loop(1, NT, ag_step, 0)
    ag_r[:, tile(t, 512)] = ag_block(t)

    zcopy(4).wait_recv()
    zcopy(6).start()
    zcopy(5).wait_recv()
    zcopy(7).start()
    label_copy.wait_recv()
    for i in range(2):
        keep[i] = keep[i] + got[4 + i]
    border = lab_r[0:1, :] + kept_off
    crossing = (rows >= border) & (cols < border)
    mask[...] = jnp.where((cols <= rows) & jnp.logical_not(crossing), 1.0, 0.0)
    dk[...] = jnp.zeros_like(dk)
    dv[...] = jnp.zeros_like(dv)
    scale = float(HD) ** (-0.5)

    def at_copy(j, d):
        peer = lax.rem(t + d, NT)
        return rcopy(
            at_s.at[j, peer], at_r.at[j, :, tile(t)],
            atsend.at[j, d - 1], atrecv.at[j, d - 1], at_t(d),
        )

    def at_got(j, d):
        source = lax.rem(t + NT - d, NT)
        return rcopy(
            at_s.at[j, source], at_r.at[j, :, tile(source)],
            atsend.at[j, d - 1], atrecv.at[j, d - 1], at_t(d),
        )

    def xcopy(j, d):
        return rcopy(
            xs.at[j, lax.rem(x + d, X)], xr.at[j, d - 1],
            xsend.at[j, d - 1], xrecv.at[j, d - 1], at_x(d),
        )

    def rcopy_z(j, d):
        return rcopy(
            zs.at[j, lax.rem(z + d, Z)], zr.at[j, d - 1],
            rsend.at[j, d - 1], rrecv.at[j, d - 1], at_z(d),
        )

    def forward_heads(j):
        def step(c, carry):
            query = keep[2 + j, :, tile(c)]
            key = keep[0, :, tile(c)]
            value = keep[1, :, tile(c)]
            allowed = mask[...] > 0.5
            score = jnp.where(allowed, dot(query, key, NTD) * scale, -1e30)
            top = jnp.max(score, axis=-1, keepdims=True)
            expo = jnp.where(allowed, jnp.exp(score - top), 0.0)
            prob = expo / jnp.sum(expo, axis=-1, keepdims=True)
            probs[c] = prob
            out = dot(prob.astype(BF), value)
            outs[c] = out.astype(BF)
            at_s[j, c] = out.T.astype(BF)
            return carry

        lax.fori_loop(0, KV, step, 0, unroll=2)

    def backward_heads(j):
        def step(c, carry):
            query = keep[2 + j, :, tile(c)]
            key = keep[0, :, tile(c)]
            value = keep[1, :, tile(c)]
            grad = ag_r[:, tile(c * GROUP + j)]
            prob = probs[c]
            delta = jnp.sum(grad.astype(F32) * outs[c].astype(F32), axis=-1, keepdims=True)
            score_grad = (prob * (dot(grad, value, NTD) - delta)).astype(BF)
            qg_ref[:, tile(c * GROUP + j)] = (dot(score_grad, key) * scale).astype(BF)
            dk[c] += dot(score_grad, query, TN)
            dv[c] += dot(prob.astype(BF), grad, TN)
            return carry

        lax.fori_loop(0, KV, step, 0, unroll=2)

    def reduce_x(j):
        for d in range(1, X):
            xcopy(j, d).wait_recv()

        def step(zz, carry):
            total = xs[j, x, :, tile(zz)].astype(F32)
            for d in range(1, X):
                total = total + xr[j, d - 1, :, tile(zz)].astype(F32)
            zs[j, zz] = total.astype(BF)
            return carry

        lax.fori_loop(0, Z, step, 0)
        for d in (4, 3, 5, 2, 6, 1, 7):
            rcopy_z(j, d).start()

    def reduce_z(j):
        total = zs[j, z].astype(F32)
        for d in range(1, Z):
            rcopy_z(j, d).wait_recv()
            total = total + zr[j, d - 1].astype(F32)
        wg_ref[j * HD : (j + 1) * HD, :] = total

    for j in range(GROUP):
        zcopy(6 + j).wait_recv()
        if j < 2:
            zcopy(8 + j).start()
        keep[2 + j] = keep[2 + j] + got[6 + j]
        forward_heads(j)
        for d in (4, 3, 5, 2, 6, 1, 7):
            at_copy(j, d).start()
        at_r[j, :, tile(t)] = at_s[j, t]
        if j > 0:
            reduce_x(j - 1)
        for d in range(1, NT):
            at_got(j, d).wait_recv()

        def weight_step(zz, carry):
            term = dot(at_r[j], gall[:, tile(zz, 512)]).astype(BF)
            for xx in range(X):
                xs[j, xx, :, tile(zz)] = term[:, xx * HD : (xx + 1) * HD]
            return carry

        lax.fori_loop(0, Z, weight_step, 0)
        for d in (2, 1, 3):
            xcopy(j, d).start()
        if j == 0:
            for d in range(1, NT):
                ag_got(d).wait_recv()
        backward_heads(j)

    for c in range(KV):
        kg_ref[:, c * HD : (c + 1) * HD] = (dk[c] * scale).astype(BF)
        vg_ref[:, c * HD : (c + 1) * HD] = dv[c].astype(BF)
    for j in range(GROUP - 1):
        reduce_z(j)
    reduce_x(GROUP - 1)

    label_copy.wait_send()
    for i in range(10):
        zcopy(i).wait_send()
    for i in range(4):
        for n in range(3):
            ycopy(i, n, t).wait_send()
            ccopy(i, n, from_t(n)).wait_send()
        ccopy(i, 3, t).wait_send()
    for d in range(1, NT):
        ag_copy(d).wait_send()
    for j in range(GROUP):
        for d in range(1, NT):
            at_copy(j, d).wait_send()
        for d in range(1, X):
            xcopy(j, d).wait_send()
    reduce_z(GROUP - 1)
    for j in range(GROUP):
        for d in range(1, Z):
            rcopy_z(j, d).wait_send()


def local(queries, keys, values, out_grad, out_weight, lengths, dest_group, dest_offset):
    dma = pltpu.SemaphoreType.DMA
    vm = pltpu.VMEM
    return pl.pallas_call(
        kernel,
        out_shape=(
            jax.ShapeDtypeStruct((T, 4096), BF),
            jax.ShapeDtypeStruct((T, 1024), BF),
            jax.ShapeDtypeStruct((T, 1024), BF),
            jax.ShapeDtypeStruct((512, 128), F32),
        ),
        in_specs=[pl.BlockSpec(memory_space=pl.ANY)] * 5 + [pl.BlockSpec(memory_space=pltpu.SMEM)] * 3,
        out_specs=tuple([pl.BlockSpec(memory_space=pltpu.VMEM)] * 4),
        scratch_shapes=[
            vm((2 * T, 10240), BF),
            vm((512, 4096), BF),
            vm((2 * T, 2 * T), BF),
            vm((T, T), F32),
            vm((8, 128), jnp.int32),
            vm((8, 128), jnp.int32),
            vm((10, T, 1024), BF),
            vm((6, T, 1024), BF),
            vm((10, T, 1024), BF),
            vm((NT * T, 4096), BF),
            vm((NT * T, 512), BF),
            vm((T, 4096), BF),
            vm((GROUP, KV, HD, T), BF),
            vm((GROUP, HD, NT * T), BF),
            vm((KV, T, T), F32),
            vm((KV, T, HD), BF),
            vm((KV, T, HD), F32),
            vm((KV, T, HD), F32),
            vm((GROUP, X, HD, 1024), BF),
            vm((GROUP, X - 1, HD, 1024), BF),
            vm((GROUP, Z, HD, 128), BF),
            vm((GROUP, Z - 1, HD, 128), BF),
            dma((9,)),
            dma((10,)), dma((10,)),
            dma((2,)),
            dma((4, 3)), dma((4, 3)),
            dma((4, 4)), dma((4, 4)),
            dma((7,)), dma((7,)),
            dma((4, 7)), dma((4, 7)),
            dma((4, 3)), dma((4, 3)),
            dma((4, 7)), dma((4, 7)),
        ],
        compiler_params=pltpu.CompilerParams(
            collective_id=0, has_side_effects=True, vmem_limit_bytes=60 * 2**20
        ),
        cost_estimate=pl.CostEstimate(flops=30_000_000_000, bytes_accessed=12_000_000, transcendentals=600_000),
    )(queries, keys, values, out_grad, out_weight, lengths, dest_group, dest_offset)


def solution(mesh):
    in_specs = (
        P(("dp", "tensor"), None, None),
        P(("dp", "tensor"), None, None),
        P(("dp", "tensor"), None, None),
        P(("dp", "tensor"), None, None),
        P("tensor", None),
        P(("dp", "tensor")),
        P(("dp", "tensor")),
        P(("dp", "tensor")),
    )
    out_specs = (
        P(("dp", "tensor"), None),
        P(("dp", "tensor"), None),
        P(("dp", "tensor"), None),
        P("tensor", "dp"),
    )
    return jax.shard_map(local, mesh=mesh, in_specs=in_specs, out_specs=out_specs, check_vma=False)
```

```python
import functools

import jax
import jax.numpy as jnp
from jax import lax
from jax.experimental import pallas as pl
from jax.experimental.pallas import tpu as pltpu
from jax.sharding import PartitionSpec as P

MESH = pl.DeviceIdType.MESH
BF = jnp.bfloat16
F32 = jnp.float32
HD = 128
T = 128
X = 4
Z = 8
NT = 8
KV = 8
GROUP = 4
NN = (((1,), (0,)), ((), ()))
NTD = (((1,), (1,)), ((), ()))
TN = (((0,), (0,)), ((), ()))
PLACE = {4: 0, 2: 1, 0: 2, 6: 3, 3: 4, 5: 5, 7: 6, 1: 7}


def dot(a, b, dims=NN):
    return lax.dot_general(a, b, dims, preferred_element_type=F32)


def tile(index, size=128):
    start = index * size
    if not isinstance(index, int):
        start = pl.multiple_of(start, size)
    return pl.ds(start, size)


def seat(c):
    return lax.rem(c, 2) * 4 + c // 2


def kernel(
    q_hbm, k_hbm, v_hbm, g_hbm, w_hbm, len_ref, grp_ref, off_ref,
    qg_ref, kg_ref, vg_ref, wg_ref,
    xin, wv, pack, mask, lab_s, lab_r,
    send, keep, got, gall,
    ag_s, ag_r, at_s, at_r, probs, outs, dk, dv,
    xs, xr, zs, zr,
    in_sem, zsend, zrecv, qsend, qrecv, lsem, ysend, yrecv, csend, crecv,
    agsend, agrecv, atsend, atrecv, xsend, xrecv, rsend, rrecv,
):
    dp = lax.axis_index("dp")
    t = lax.axis_index("tensor")
    z = dp // X
    x = dp % X

    def at_z(d):
        return (lax.rem(z + d, Z) * X + x, t)

    def at_x(d):
        return (z * X + lax.rem(x + d, X), t)

    def at_t(d):
        return (dp, lax.rem(t + d, NT))

    partner = at_z(Z // 2)
    sibling_t = t + 1 - 2 * lax.rem(t, 2)
    sibling = (dp, sibling_t)

    def rcopy(src, dst, ssem, rsem, device):
        return pltpu.make_async_remote_copy(
            src_ref=src, dst_ref=dst, send_sem=ssem, recv_sem=rsem,
            device_id=device, device_id_type=MESH,
        )

    barrier = pltpu.get_barrier_semaphore()
    peers = [at_z(d) for d in range(1, Z)] + [at_x(d) for d in range(1, X)]
    peers = peers + [at_t(d) for d in range(1, NT)]
    for peer in peers:
        pl.semaphore_signal(barrier, inc=1, device_id=peer, device_id_type=MESH)

    loads = []
    for hbm, start, width in ((g_hbm, 0, 4096), (k_hbm, 4096, 1024), (v_hbm, 5120, 1024), (q_hbm, 6144, 4096)):
        for slot in range(2):
            loads.append(
                pltpu.make_async_copy(
                    hbm.at[slot],
                    xin.at[slot * T : (slot + 1) * T, start : start + width],
                    in_sem.at[len(loads)],
                )
            )
    loads.append(pltpu.make_async_copy(w_hbm, wv, in_sem.at[len(loads)]))
    for load in loads:
        load.start()

    rows = lax.broadcasted_iota(jnp.int32, (T, T), 0)
    cols = lax.broadcasted_iota(jnp.int32, (T, T), 1)
    moved_off = jnp.int32(0)
    kept_off = jnp.int32(0)
    for slot in range(2):
        length = len_ref[slot]
        offset = off_ref[slot]
        moving = jnp.where(grp_ref[slot] != dp, 1, 0)
        hit = jnp.where((cols < length) & (rows == cols + offset), 1.0, 0.0)
        went = moving.astype(F32)
        pack[0:T, slot * T : (slot + 1) * T] = (hit * went).astype(BF)
        pack[T : 2 * T, slot * T : (slot + 1) * T] = (hit * (1.0 - went)).astype(BF)
        moved_off = moved_off + moving * offset
        kept_off = kept_off + (1 - moving) * offset
    lab_s[...] = jnp.zeros((8, 128), jnp.int32) + moved_off

    def zcopy(i):
        return rcopy(send.at[i], got.at[i], zsend.at[i], zrecv.at[i], partner)

    def qcopy(j, p):
        lanes = slice(p * 512, (p + 1) * 512)
        return rcopy(
            send.at[6 + j, :, lanes], got.at[6 + j, :, lanes], qsend.at[j, p], qrecv.at[j, p], partner
        )

    def start_q(j):
        for p in range(2):
            qcopy(j, p).start()

    label_copy = rcopy(lab_s, lab_r, lsem.at[0], lsem.at[1], partner)

    def packed(start):
        return dot(pack[...], xin[:, pl.ds(pl.multiple_of(start, 512), 512)])

    loads[0].wait()
    loads[1].wait()
    own_rows = tile(t)
    for i in range(4):
        for half in range(2):
            both = packed(i * 1024 + half * 512).astype(BF)
            send[i, :, half * 512 : (half + 1) * 512] = both[0:T]
            gall[own_rows, i * 1024 + half * 512 : i * 1024 + (half + 1) * 512] = both[T:]
        if i == 0:
            pl.semaphore_wait(barrier, len(peers))
            label_copy.start()
            zcopy(0).start()
        if i == 1:
            zcopy(1).start()
    for load in loads[2:8]:
        load.wait()
    for i in range(2):
        for half in range(2):
            both = packed(4096 + i * 1024 + half * 512).astype(BF)
            send[4 + i, :, half * 512 : (half + 1) * 512] = both[0:T]
            keep[i, :, half * 512 : (half + 1) * 512] = both[T:]

    def pack_q(c, carry):
        both = packed(6144 + c * 512).astype(BF)
        for j in range(GROUP):
            part = both[:, j * HD : (j + 1) * HD]
            send[6 + j, :, tile(seat(c))] = part[0:T]
            keep[2 + j, :, tile(seat(c))] = part[T:]
        return carry

    lax.fori_loop(0, KV, pack_q, 0)

    def block(i, row_t):
        return gall.at[tile(row_t), i * 1024 : (i + 1) * 1024]

    def ycopy(i, n, row_t):
        return rcopy(block(i, row_t), block(i, row_t), ysend.at[i, n], yrecv.at[i, n], at_t(2 * (n + 1)))

    def ccopy(i, n, row_t):
        return rcopy(block(i, row_t), block(i, row_t), csend.at[i, n], crecv.at[i, n], sibling)

    def from_t(n):
        return lax.rem(t + NT - 2 * (n + 1), NT)

    def sib_from_t(n):
        return lax.rem(sibling_t + NT - 2 * (n + 1), NT)

    def forward(i):
        for n in (0, 2, 1):
            ycopy(i, n, from_t(n)).wait_recv()
            ccopy(i, n, from_t(n)).start()

    for i in range(4):
        zcopy(i).wait_recv()
        zcopy(i + 2).start()
        lanes = slice(i * 1024, (i + 1) * 1024)
        gall[own_rows, lanes] = gall[own_rows, lanes] + got[i]
        for n in (1, 0, 2):
            ycopy(i, n, t).start()
        ccopy(i, 3, t).start()
        if i > 0:
            forward(i - 1)
    forward(3)
    loads[8].wait()
    for i in range(4):
        for n in range(3):
            ccopy(i, n, sib_from_t(n)).wait_recv()
        ccopy(i, 3, sibling_t).wait_recv()

    zcopy(4).wait_recv()
    start_q(0)

    def ag_copy(d):
        peer = lax.rem(t + d, NT)
        return rcopy(
            ag_s.at[tile(peer), :], ag_r.at[:, tile(t, 512)],
            agsend.at[d - 1], agrecv.at[d - 1], at_t(d),
        )

    def ag_got(d):
        source = lax.rem(t + NT - d, NT)
        return rcopy(
            ag_s.at[tile(source), :], ag_r.at[:, tile(source, 512)],
            agsend.at[d - 1], agrecv.at[d - 1], at_t(d),
        )

    def ag_block(peer):
        return dot(gall[tile(peer), :], wv[...], NTD).astype(BF)

    def ag_step(d, carry):
        peer = lax.rem(t + d, NT)
        ag_s[tile(peer), :] = ag_block(peer)
        ag_copy(d).start()
        return carry

    lax.fori_loop(1, NT, ag_step, 0)
    ag_r[:, tile(t, 512)] = ag_block(t)

    zcopy(5).wait_recv()
    start_q(1)
    label_copy.wait_recv()
    for i in range(2):
        keep[i] = keep[i] + got[4 + i]
    border = lab_r[0:1, :] + kept_off
    crossing = (rows >= border) & (cols < border)
    mask[...] = jnp.where((cols <= rows) & jnp.logical_not(crossing), 1.0, 0.0)
    dk[...] = jnp.zeros_like(dk)
    dv[...] = jnp.zeros_like(dv)
    scale = float(HD) ** (-0.5)

    def at_copy(j, d):
        peer = lax.rem(t + d, NT)
        return rcopy(
            at_s.at[j, peer], at_r.at[j, :, tile(t)],
            atsend.at[j, d - 1], atrecv.at[j, d - 1], at_t(d),
        )

    def at_got(j, d):
        source = lax.rem(t + NT - d, NT)
        return rcopy(
            at_s.at[j, source], at_r.at[j, :, tile(source)],
            atsend.at[j, d - 1], atrecv.at[j, d - 1], at_t(d),
        )

    def distance(half, k):
        return lax.rem(4 + 6 * k, Z) if half == 0 else lax.rem(3 + 2 * k, Z)

    def xcopy(j, half, d):
        lanes = slice(half * 512, (half + 1) * 512)
        return rcopy(
            xs.at[j, lax.rem(x + d, X), :, lanes], xr.at[j, d - 1, :, lanes],
            xsend.at[j, half, d - 1], xrecv.at[j, half, d - 1], at_x(d),
        )

    def rcopy_z(j, d):
        return rcopy(
            zs.at[j, PLACE[d]], zr.at[j, d - 1],
            rsend.at[j, d - 1], rrecv.at[j, d - 1], at_z(d),
        )

    def send_attended(j, p):
        def step(m, carry):
            peer = 2 * m + p

            @pl.when(peer != t)
            def _():
                at_copy(j, lax.rem(peer + NT - t, NT)).start()

            return carry

        lax.fori_loop(0, 4, step, 0)

    def forward_heads(j, p):
        def step(m, carry):
            c = 2 * m + p
            query = keep[2 + j, :, tile(p * 4 + m)]
            key = keep[0, :, tile(c)]
            value = keep[1, :, tile(c)]
            allowed = mask[...] > 0.5
            score = jnp.where(allowed, dot(query, key, NTD) * scale, -1e30)
            top = jnp.max(score, axis=-1, keepdims=True)
            expo = jnp.exp(score - top)
            prob = expo / jnp.sum(expo, axis=-1, keepdims=True)
            probs[c] = prob
            out = dot(prob.astype(BF), value)
            out = out.astype(BF)
            outs[c] = out
            at_s[j, c] = out.T
            return carry

        lax.fori_loop(0, 4, step, 0, unroll=4)

    def backward_heads(j):
        def step(c, carry):
            query = keep[2 + j, :, tile(seat(c))]
            key = keep[0, :, tile(c)]
            value = keep[1, :, tile(c)]
            grad = ag_r[:, tile(c * GROUP + j)]
            prob = probs[c]
            delta = jnp.sum(grad.astype(F32) * outs[c].astype(F32), axis=-1, keepdims=True)
            score_grad = (prob * (dot(grad, value, NTD) - delta)).astype(BF)
            qg_ref[:, tile(c * GROUP + j)] = (dot(score_grad, key) * scale).astype(BF)
            dk[c] += dot(score_grad, query, TN)
            dv[c] += dot(prob.astype(BF), grad, TN)
            return carry

        lax.fori_loop(0, KV, step, 0, unroll=4)

    def reduce_x(j, half):
        for d in range(1, X):
            xcopy(j, half, d).wait_recv()

        def step(k, carry):
            place = half * 4 + k
            total = xs[j, x, :, tile(place)].astype(F32)
            for d in range(1, X):
                total = total + xr[j, d - 1, :, tile(place)].astype(F32)
            zs[j, place] = total.astype(BF)
            return carry

        lax.fori_loop(0, 4, step, 0)

    def send_z(j, half):
        for d in ((4, 2, 6), (3, 5, 1, 7))[half]:
            rcopy_z(j, d).start()

    def reduce_z(j):
        total = zs[j, PLACE[0]].astype(F32)
        for d in (4, 2, 6, 3, 5, 1, 7):
            rcopy_z(j, d).wait_recv()
            total = total + zr[j, d - 1].astype(F32)
        wg_ref[j * HD : (j + 1) * HD, :] = total

    def weight_term(j, half):
        def step(k, carry):
            place = half * 4 + k
            zz = lax.rem(z + distance(half, k), Z)
            term = dot(at_r[j], gall[:, tile(zz, 512)]).astype(BF)
            for xx in range(X):
                xs[j, xx, :, tile(place)] = term[:, xx * HD : (xx + 1) * HD]
            return carry

        lax.fori_loop(0, 4, step, 0)
        for d in (2, 1, 3):
            xcopy(j, half, d).start()

    last = GROUP - 1
    for j in range(GROUP):
        for p in range(2):
            qcopy(j, p).wait_recv()
            if p == 1 and j < 2:
                start_q(j + 2)
            lanes = slice(p * 512, (p + 1) * 512)
            keep[2 + j, :, lanes] = keep[2 + j, :, lanes] + got[6 + j, :, lanes]
            forward_heads(j, p)
            send_attended(j, p)
        at_r[j, :, tile(t)] = at_s[j, t]
        if j == 0:
            for d in range(1, NT):
                ag_got(d).wait_recv()
        if j == last:
            for i in range(last - 1):
                for half in range(2):
                    send_z(i, half)
        backward_heads(j)
        for d in range(1, NT):
            at_got(j, d).wait_recv()
        for half in range(2):
            weight_term(j, half)
        if j > 0:
            for half in range(2):
                reduce_x(j - 1, half)
                if j == last:
                    send_z(j - 1, half)

    for c in range(KV):
        kg_ref[:, c * HD : (c + 1) * HD] = (dk[c] * scale).astype(BF)
        vg_ref[:, c * HD : (c + 1) * HD] = dv[c].astype(BF)
    for half in range(2):
        reduce_x(last, half)
        send_z(last, half)
    for j in range(last):
        reduce_z(j)

    label_copy.wait_send()
    for i in range(6):
        zcopy(i).wait_send()
    for j in range(GROUP):
        for p in range(2):
            qcopy(j, p).wait_send()
    for i in range(4):
        for n in range(3):
            ycopy(i, n, t).wait_send()
            ccopy(i, n, from_t(n)).wait_send()
        ccopy(i, 3, t).wait_send()
    for d in range(1, NT):
        ag_copy(d).wait_send()
    for j in range(GROUP):
        for d in range(1, NT):
            at_copy(j, d).wait_send()
        for half in range(2):
            for d in range(1, X):
                xcopy(j, half, d).wait_send()
    reduce_z(GROUP - 1)
    for j in range(GROUP):
        for d in range(1, Z):
            rcopy_z(j, d).wait_send()


def deliver(*refs):
    count = len(refs) // 2
    for source, target in zip(refs[:count], refs[count:]):
        target[...] = source[...]


def local(queries, keys, values, out_grad, out_weight, lengths, dest_group, dest_offset):
    dma = pltpu.SemaphoreType.DMA
    vm = pltpu.VMEM
    results = pl.pallas_call(
        kernel,
        out_shape=(
            jax.ShapeDtypeStruct((T, 4096), BF),
            jax.ShapeDtypeStruct((T, 1024), BF),
            jax.ShapeDtypeStruct((T, 1024), BF),
            jax.ShapeDtypeStruct((512, 128), F32),
        ),
        in_specs=[pl.BlockSpec(memory_space=pl.ANY)] * 5 + [pl.BlockSpec(memory_space=pltpu.SMEM)] * 3,
        out_specs=tuple([pl.BlockSpec(memory_space=pltpu.VMEM)] * 4),
        scratch_shapes=[
            vm((2 * T, 10240), BF),
            vm((512, 4096), BF),
            vm((2 * T, 2 * T), BF),
            vm((T, T), F32),
            vm((8, 128), jnp.int32),
            vm((8, 128), jnp.int32),
            vm((10, T, 1024), BF),
            vm((6, T, 1024), BF),
            vm((10, T, 1024), BF),
            vm((NT * T, 4096), BF),
            vm((NT * T, 512), BF),
            vm((T, 4096), BF),
            vm((GROUP, KV, HD, T), BF),
            vm((GROUP, HD, NT * T), BF),
            vm((KV, T, T), F32),
            vm((KV, T, HD), BF),
            vm((KV, T, HD), F32),
            vm((KV, T, HD), F32),
            vm((GROUP, X, HD, 1024), BF),
            vm((GROUP, X - 1, HD, 1024), BF),
            vm((GROUP, Z, HD, 128), BF),
            vm((GROUP, Z - 1, HD, 128), BF),
            dma((9,)),
            dma((6,)), dma((6,)),
            dma((4, 2)), dma((4, 2)),
            dma((2,)),
            dma((4, 3)), dma((4, 3)),
            dma((4, 4)), dma((4, 4)),
            dma((7,)), dma((7,)),
            dma((4, 7)), dma((4, 7)),
            dma((4, 2, 3)), dma((4, 2, 3)),
            dma((4, 7)), dma((4, 7)),
        ],
        compiler_params=pltpu.CompilerParams(
            collective_id=0, has_side_effects=True, vmem_limit_bytes=60 * 2**20
        ),
        cost_estimate=pl.CostEstimate(flops=30_000_000_000, bytes_accessed=12_000_000, transcendentals=600_000),
    )(queries, keys, values, out_grad, out_weight, lengths, dest_group, dest_offset)
    specs = [pl.BlockSpec((r.shape[0] // 4, r.shape[1]), lambda i: (i, 0)) for r in results]
    return pl.pallas_call(
        deliver,
        grid=(4,),
        out_shape=tuple(jax.ShapeDtypeStruct(r.shape, r.dtype) for r in results),
        in_specs=specs,
        out_specs=tuple(specs),
    )(*results)


def solution(mesh):
    in_specs = (
        P(("dp", "tensor"), None, None),
        P(("dp", "tensor"), None, None),
        P(("dp", "tensor"), None, None),
        P(("dp", "tensor"), None, None),
        P("tensor", None),
        P(("dp", "tensor")),
        P(("dp", "tensor")),
        P(("dp", "tensor")),
    )
    out_specs = (
        P(("dp", "tensor"), None),
        P(("dp", "tensor"), None),
        P(("dp", "tensor"), None),
        P("tensor", "dp"),
    )
    return jax.shard_map(local, mesh=mesh, in_specs=in_specs, out_specs=out_specs, check_vma=False)
```

```python
import functools

import jax
import jax.numpy as jnp
from jax import lax
from jax.experimental import pallas as pl
from jax.experimental.pallas import tpu as pltpu
from jax.sharding import PartitionSpec as P

MESH = pl.DeviceIdType.MESH
BF = jnp.bfloat16
F32 = jnp.float32
HD = 128
T = 128
X = 4
Z = 8
NT = 8
KV = 8
GROUP = 4
NN = (((1,), (0,)), ((), ()))
NTD = (((1,), (1,)), ((), ()))
TN = (((0,), (0,)), ((), ()))
PLACE = {4: 0, 2: 1, 0: 2, 6: 3, 3: 4, 5: 5, 7: 6, 1: 7}


def dot(a, b, dims=NN):
    return lax.dot_general(a, b, dims, preferred_element_type=F32)


def tile(index, size=128):
    start = index * size
    if not isinstance(index, int):
        start = pl.multiple_of(start, size)
    return pl.ds(start, size)


def seat(c):
    return lax.rem(c, 2) * 4 + c // 2


def kernel(
    q_hbm, k_hbm, v_hbm, g_hbm, w_hbm, len_ref, grp_ref, off_ref,
    qg_ref, kg_ref, vg_ref, wg_ref,
    xin, wv, pack, mask, lab_s, lab_r,
    send, keep, got, gall,
    ag_s, ag_r, at_s, at_r, probs, outs, dk, dv,
    xs, xa, xr, zs, zr,
    in_sem, zsend, zrecv, qsend, qrecv, lsem, ysend, yrecv, csend, crecv,
    agsend, agrecv, atsend, atrecv, asend, arecv, xsend, xrecv, rsend, rrecv,
):
    dp = lax.axis_index("dp")
    t = lax.axis_index("tensor")
    z = dp // X
    x = dp % X

    def at_z(d):
        return (lax.rem(z + d, Z) * X + x, t)

    def at_x(d):
        return (z * X + lax.rem(x + d, X), t)

    def at_t(d):
        return (dp, lax.rem(t + d, NT))

    partner = at_z(Z // 2)
    sibling_t = t + 1 - 2 * lax.rem(t, 2)
    sibling = (dp, sibling_t)

    def rcopy(src, dst, ssem, rsem, device):
        return pltpu.make_async_remote_copy(
            src_ref=src, dst_ref=dst, send_sem=ssem, recv_sem=rsem,
            device_id=device, device_id_type=MESH,
        )

    barrier = pltpu.get_barrier_semaphore()
    peers = [at_z(d) for d in range(1, Z)] + [at_x(d) for d in range(1, X)]
    peers = peers + [at_t(d) for d in range(1, NT)]
    for peer in peers:
        pl.semaphore_signal(barrier, inc=1, device_id=peer, device_id_type=MESH)

    loads = []
    for hbm, start, width in ((g_hbm, 0, 4096), (k_hbm, 4096, 1024), (v_hbm, 5120, 1024), (q_hbm, 6144, 4096)):
        for slot in range(2):
            loads.append(
                pltpu.make_async_copy(
                    hbm.at[slot],
                    xin.at[slot * T : (slot + 1) * T, start : start + width],
                    in_sem.at[len(loads)],
                )
            )
    loads.append(pltpu.make_async_copy(w_hbm, wv, in_sem.at[len(loads)]))
    for load in loads:
        load.start()

    rows = lax.broadcasted_iota(jnp.int32, (T, T), 0)
    cols = lax.broadcasted_iota(jnp.int32, (T, T), 1)
    moved_off = jnp.int32(0)
    kept_off = jnp.int32(0)
    for slot in range(2):
        length = len_ref[slot]
        offset = off_ref[slot]
        moving = jnp.where(grp_ref[slot] != dp, 1, 0)
        hit = jnp.where((cols < length) & (rows == cols + offset), 1.0, 0.0)
        went = moving.astype(F32)
        pack[0:T, slot * T : (slot + 1) * T] = (hit * went).astype(BF)
        pack[T : 2 * T, slot * T : (slot + 1) * T] = (hit * (1.0 - went)).astype(BF)
        moved_off = moved_off + moving * offset
        kept_off = kept_off + (1 - moving) * offset
    lab_s[...] = jnp.zeros((8, 128), jnp.int32) + moved_off

    def zcopy(i):
        return rcopy(send.at[i], got.at[i], zsend.at[i], zrecv.at[i], partner)

    def qcopy(j, p):
        lanes = slice(p * 512, (p + 1) * 512)
        return rcopy(
            send.at[6 + j, :, lanes], got.at[6 + j, :, lanes], qsend.at[j, p], qrecv.at[j, p], partner
        )

    def start_q(j):
        for p in range(2):
            qcopy(j, p).start()

    label_copy = rcopy(lab_s, lab_r, lsem.at[0], lsem.at[1], partner)

    def packed(start):
        return dot(pack[...], xin[:, pl.ds(pl.multiple_of(start, 512), 512)])

    loads[0].wait()
    loads[1].wait()
    own_rows = tile(t)
    for i in range(4):
        for half in range(2):
            both = packed(i * 1024 + half * 512).astype(BF)
            send[i, :, half * 512 : (half + 1) * 512] = both[0:T]
            gall[own_rows, i * 1024 + half * 512 : i * 1024 + (half + 1) * 512] = both[T:]
        if i == 0:
            pl.semaphore_wait(barrier, len(peers))
            label_copy.start()
            zcopy(0).start()
        if i == 1:
            zcopy(1).start()
    for load in loads[2:8]:
        load.wait()
    for i in range(2):
        for half in range(2):
            both = packed(4096 + i * 1024 + half * 512).astype(BF)
            send[4 + i, :, half * 512 : (half + 1) * 512] = both[0:T]
            keep[i, :, half * 512 : (half + 1) * 512] = both[T:]

    def pack_q(c, carry):
        both = packed(6144 + c * 512).astype(BF)
        for j in range(GROUP):
            part = both[:, j * HD : (j + 1) * HD]
            send[6 + j, :, tile(seat(c))] = part[0:T]
            keep[2 + j, :, tile(seat(c))] = part[T:]
        return carry

    lax.fori_loop(0, KV, pack_q, 0)

    def block(i, row_t):
        return gall.at[tile(row_t), i * 1024 : (i + 1) * 1024]

    def ycopy(i, n, row_t):
        return rcopy(block(i, row_t), block(i, row_t), ysend.at[i, n], yrecv.at[i, n], at_t(2 * (n + 1)))

    def ccopy(i, n, row_t):
        return rcopy(block(i, row_t), block(i, row_t), csend.at[i, n], crecv.at[i, n], sibling)

    def from_t(n):
        return lax.rem(t + NT - 2 * (n + 1), NT)

    def sib_from_t(n):
        return lax.rem(sibling_t + NT - 2 * (n + 1), NT)

    def forward(i):
        for n in (0, 2, 1):
            ycopy(i, n, from_t(n)).wait_recv()
            ccopy(i, n, from_t(n)).start()

    for i in range(4):
        zcopy(i).wait_recv()
        zcopy(i + 2).start()
        lanes = slice(i * 1024, (i + 1) * 1024)
        gall[own_rows, lanes] = gall[own_rows, lanes] + got[i]
        for n in (1, 0, 2):
            ycopy(i, n, t).start()
        ccopy(i, 3, t).start()
        if i > 0:
            forward(i - 1)
    forward(3)
    loads[8].wait()
    for i in range(4):
        for n in range(3):
            ccopy(i, n, sib_from_t(n)).wait_recv()
        ccopy(i, 3, sibling_t).wait_recv()

    zcopy(4).wait_recv()
    start_q(0)

    def ag_copy(d):
        peer = lax.rem(t + d, NT)
        return rcopy(
            ag_s.at[tile(peer), :], ag_r.at[:, tile(t, 512)],
            agsend.at[d - 1], agrecv.at[d - 1], at_t(d),
        )

    def ag_got(d):
        source = lax.rem(t + NT - d, NT)
        return rcopy(
            ag_s.at[tile(source), :], ag_r.at[:, tile(source, 512)],
            agsend.at[d - 1], agrecv.at[d - 1], at_t(d),
        )

    def ag_block(peer):
        return dot(gall[tile(peer), :], wv[...], NTD).astype(BF)

    def ag_step(d, carry):
        peer = lax.rem(t + d, NT)
        ag_s[tile(peer), :] = ag_block(peer)
        ag_copy(d).start()
        return carry

    lax.fori_loop(1, NT, ag_step, 0)
    ag_r[:, tile(t, 512)] = ag_block(t)

    zcopy(5).wait_recv()
    start_q(1)
    label_copy.wait_recv()
    for i in range(2):
        keep[i] = keep[i] + got[4 + i]
    border = lab_r[0:1, :] + kept_off
    crossing = (rows >= border) & (cols < border)
    mask[...] = jnp.where((cols <= rows) & jnp.logical_not(crossing), 1.0, 0.0)
    dk[...] = jnp.zeros_like(dk)
    dv[...] = jnp.zeros_like(dv)
    scale = float(HD) ** (-0.5)

    def at_copy(j, d):
        peer = lax.rem(t + d, NT)
        return rcopy(
            at_s.at[j, peer], at_r.at[j, :, tile(t)],
            atsend.at[j, d - 1], atrecv.at[j, d - 1], at_t(d),
        )

    def at_got(j, d):
        source = lax.rem(t + NT - d, NT)
        return rcopy(
            at_s.at[j, source], at_r.at[j, :, tile(source)],
            atsend.at[j, d - 1], atrecv.at[j, d - 1], at_t(d),
        )

    def distance(half, k):
        return lax.rem(4 + 6 * k, Z) if half == 0 else lax.rem(3 + 2 * k, Z)

    def rows_of(r):
        return slice(r * 64, (r + 1) * 64)

    def lanes_of(half):
        return slice(half * 512, (half + 1) * 512)

    def beside(s):
        return lax.rem(x + 1 + 2 * s, X)

    def relay_copy(j, half, s):
        return rcopy(
            xs.at[j, lax.rem(x + 2, X), rows_of(s), lanes_of(half)], xa.at[j, s, :, lanes_of(half)],
            asend.at[j, half, s], arecv.at[j, half, s], at_x(1 + 2 * s),
        )

    def xcopy(j, half, s, r):
        return rcopy(
            xs.at[j, beside(s), rows_of(r), lanes_of(half)], xr.at[j, s, rows_of(r), lanes_of(half)],
            xsend.at[j, half, s, r], xrecv.at[j, half, s, r], at_x(1 + 2 * s),
        )

    def rcopy_z(j, d):
        return rcopy(
            zs.at[j, PLACE[d]], zr.at[j, d - 1],
            rsend.at[j, d - 1], rrecv.at[j, d - 1], at_z(d),
        )

    def send_attended(j, p):
        def step(m, carry):
            peer = 2 * m + p

            @pl.when(peer != t)
            def _():
                at_copy(j, lax.rem(peer + NT - t, NT)).start()

            return carry

        lax.fori_loop(0, 4, step, 0)

    def forward_heads(j, p):
        four = range(4)
        allowed = mask[...] > 0.5
        scores = [
            dot(keep[2 + j, :, tile(p * 4 + m)], keep[0, :, tile(2 * m + p)], NTD) * scale for m in four
        ]
        scores = [jnp.where(allowed, score, -1e30) for score in scores]
        tops = [jnp.max(score, axis=-1, keepdims=True) for score in scores]
        expos = [jnp.exp(scores[m] - tops[m]) for m in four]
        sums = [jnp.sum(expo, axis=-1, keepdims=True) for expo in expos]
        prob = [expos[m] / sums[m] for m in four]
        out = [dot(prob[m].astype(BF), keep[1, :, tile(2 * m + p)]).astype(BF) for m in four]
        for m in four:
            at_s[j, 2 * m + p] = out[m].T
        for m in four:
            probs[2 * m + p] = prob[m]
            outs[2 * m + p] = out[m]

    def backward_heads(j):
        def step(p, carry):
            four = range(4)
            heads = [2 * m + p for m in four]
            query = [keep[2 + j, :, tile(p * 4 + m)] for m in four]
            key = [keep[0, :, tile(c)] for c in heads]
            value = [keep[1, :, tile(c)] for c in heads]
            grad = [ag_r[:, tile(c * GROUP + j)] for c in heads]
            prob = [probs[c] for c in heads]
            delta = [
                jnp.sum(grad[m].astype(F32) * outs[heads[m]].astype(F32), axis=-1, keepdims=True) for m in four
            ]
            prob_grad = [dot(grad[m], value[m], NTD) for m in four]
            score_grad = [(prob[m] * (prob_grad[m] - delta[m])).astype(BF) for m in four]
            query_grad = [(dot(score_grad[m], key[m]) * scale).astype(BF) for m in four]
            key_grad = [dk[heads[m]] + dot(score_grad[m], query[m], TN) for m in four]
            value_grad = [dv[heads[m]] + dot(prob[m].astype(BF), grad[m], TN) for m in four]
            for m in four:
                qg_ref[:, tile(heads[m] * GROUP + j)] = query_grad[m]
                dk[heads[m]] = key_grad[m]
                dv[heads[m]] = value_grad[m]
            return carry

        lax.fori_loop(0, 2, step, 0)

    def relay_x(j, half):
        lanes = lanes_of(half)
        for s in range(2):
            relay_copy(j, half, s).wait_recv()
            mine = xs[j, beside(s), rows_of(s), lanes].astype(F32)
            xs[j, beside(s), rows_of(s), lanes] = (mine + xa[j, s, :, lanes].astype(F32)).astype(BF)
            xcopy(j, half, s, s).start()

    def reduce_x(j, half):
        for s in range(2):
            xcopy(j, half, s, 1 - s).wait_recv()
        for s in range(2):
            xcopy(j, half, s, s).wait_recv()

        def step(k, carry):
            place = half * 4 + k
            total = xs[j, x, :, tile(place)].astype(F32)
            for s in range(2):
                total = total + xr[j, s, :, tile(place)].astype(F32)
            zs[j, place] = total.astype(BF)
            return carry

        lax.fori_loop(0, 4, step, 0)

    def send_z(j, half):
        for d in ((4, 2, 6), (3, 5, 1, 7))[half]:
            rcopy_z(j, d).start()

    def reduce_z(j):
        total = zs[j, PLACE[0]].astype(F32)
        for d in (4, 2, 6, 3, 5, 1, 7):
            rcopy_z(j, d).wait_recv()
            total = total + zr[j, d - 1].astype(F32)
        wg_ref[j * HD : (j + 1) * HD, :] = total

    def weight_term(j, half):
        def step(k, carry):
            place = half * 4 + k
            zz = lax.rem(z + distance(half, k), Z)
            term = dot(at_r[j], gall[:, tile(zz, 512)]).astype(BF)
            for xx in range(X):
                xs[j, xx, :, tile(place)] = term[:, xx * HD : (xx + 1) * HD]
            return carry

        lax.fori_loop(0, 4, step, 0)
        for s in range(2):
            relay_copy(j, half, s).start()
        for s in range(2):
            xcopy(j, half, s, 1 - s).start()

    last = GROUP - 1
    for j in range(GROUP):
        for p in range(2):
            qcopy(j, p).wait_recv()
            if p == 1 and j < 2:
                start_q(j + 2)
            lanes = slice(p * 512, (p + 1) * 512)
            keep[2 + j, :, lanes] = keep[2 + j, :, lanes] + got[6 + j, :, lanes]
            forward_heads(j, p)
            send_attended(j, p)
        at_r[j, :, tile(t)] = at_s[j, t]
        if j == 0:
            for d in range(1, NT):
                ag_got(d).wait_recv()
        if j == last:
            for i in range(last - 1):
                for half in range(2):
                    send_z(i, half)
        if j > 0:
            for half in range(2):
                relay_x(j - 1, half)
        backward_heads(j)
        for d in range(1, NT):
            at_got(j, d).wait_recv()
        for half in range(2):
            weight_term(j, half)
        if j > 0:
            for half in range(2):
                reduce_x(j - 1, half)
                if j == last:
                    send_z(j - 1, half)

    for half in range(2):
        relay_x(last, half)
    for c in range(KV):
        kg_ref[:, c * HD : (c + 1) * HD] = (dk[c] * scale).astype(BF)
        vg_ref[:, c * HD : (c + 1) * HD] = dv[c].astype(BF)
    for half in range(2):
        reduce_x(last, half)
        send_z(last, half)
    for j in range(last):
        reduce_z(j)

    label_copy.wait_send()
    for i in range(6):
        zcopy(i).wait_send()
    for j in range(GROUP):
        for p in range(2):
            qcopy(j, p).wait_send()
    for i in range(4):
        for n in range(3):
            ycopy(i, n, t).wait_send()
            ccopy(i, n, from_t(n)).wait_send()
        ccopy(i, 3, t).wait_send()
    for d in range(1, NT):
        ag_copy(d).wait_send()
    for j in range(GROUP):
        for d in range(1, NT):
            at_copy(j, d).wait_send()
        for half in range(2):
            for s in range(2):
                relay_copy(j, half, s).wait_send()
                for r in range(2):
                    xcopy(j, half, s, r).wait_send()
    reduce_z(GROUP - 1)
    for j in range(GROUP):
        for d in range(1, Z):
            rcopy_z(j, d).wait_send()


def deliver(*refs):
    count = len(refs) // 2
    for source, target in zip(refs[:count], refs[count:]):
        target[...] = source[...]


def local(queries, keys, values, out_grad, out_weight, lengths, dest_group, dest_offset):
    dma = pltpu.SemaphoreType.DMA
    vm = pltpu.VMEM
    results = pl.pallas_call(
        kernel,
        out_shape=(
            jax.ShapeDtypeStruct((T, 4096), BF),
            jax.ShapeDtypeStruct((T, 1024), BF),
            jax.ShapeDtypeStruct((T, 1024), BF),
            jax.ShapeDtypeStruct((512, 128), F32),
        ),
        in_specs=[pl.BlockSpec(memory_space=pl.ANY)] * 5 + [pl.BlockSpec(memory_space=pltpu.SMEM)] * 3,
        out_specs=tuple([pl.BlockSpec(memory_space=pltpu.VMEM)] * 4),
        scratch_shapes=[
            vm((2 * T, 10240), BF),
            vm((512, 4096), BF),
            vm((2 * T, 2 * T), BF),
            vm((T, T), F32),
            vm((8, 128), jnp.int32),
            vm((8, 128), jnp.int32),
            vm((10, T, 1024), BF),
            vm((6, T, 1024), BF),
            vm((10, T, 1024), BF),
            vm((NT * T, 4096), BF),
            vm((NT * T, 512), BF),
            vm((T, 4096), BF),
            vm((GROUP, KV, HD, T), BF),
            vm((GROUP, HD, NT * T), BF),
            vm((KV, T, T), F32),
            vm((KV, T, HD), BF),
            vm((KV, T, HD), F32),
            vm((KV, T, HD), F32),
            vm((GROUP, X, HD, 1024), BF),
            vm((GROUP, 2, HD // 2, 1024), BF),
            vm((GROUP, 2, HD, 1024), BF),
            vm((GROUP, Z, HD, 128), BF),
            vm((GROUP, Z - 1, HD, 128), BF),
            dma((9,)),
            dma((6,)), dma((6,)),
            dma((4, 2)), dma((4, 2)),
            dma((2,)),
            dma((4, 3)), dma((4, 3)),
            dma((4, 4)), dma((4, 4)),
            dma((7,)), dma((7,)),
            dma((4, 7)), dma((4, 7)),
            dma((4, 2, 2)), dma((4, 2, 2)),
            dma((4, 2, 2, 2)), dma((4, 2, 2, 2)),
            dma((4, 7)), dma((4, 7)),
        ],
        compiler_params=pltpu.CompilerParams(
            collective_id=0, has_side_effects=True, vmem_limit_bytes=60 * 2**20
        ),
        cost_estimate=pl.CostEstimate(flops=30_000_000_000, bytes_accessed=12_000_000, transcendentals=600_000),
    )(queries, keys, values, out_grad, out_weight, lengths, dest_group, dest_offset)
    specs = [pl.BlockSpec((r.shape[0] // 4, r.shape[1]), lambda i: (i, 0)) for r in results]
    return pl.pallas_call(
        deliver,
        grid=(4,),
        out_shape=tuple(jax.ShapeDtypeStruct(r.shape, r.dtype) for r in results),
        in_specs=specs,
        out_specs=tuple(specs),
    )(*results)


def solution(mesh):
    in_specs = (
        P(("dp", "tensor"), None, None),
        P(("dp", "tensor"), None, None),
        P(("dp", "tensor"), None, None),
        P(("dp", "tensor"), None, None),
        P("tensor", None),
        P(("dp", "tensor")),
        P(("dp", "tensor")),
        P(("dp", "tensor")),
    )
    out_specs = (
        P(("dp", "tensor"), None),
        P(("dp", "tensor"), None),
        P(("dp", "tensor"), None),
        P("tensor", "dp"),
    )
    return jax.shard_map(local, mesh=mesh, in_specs=in_specs, out_specs=out_specs, check_vma=False)
```

```python
import functools

import jax
import jax.numpy as jnp
from jax import lax
from jax.experimental import pallas as pl
from jax.experimental.pallas import tpu as pltpu
from jax.sharding import PartitionSpec as P

MESH = pl.DeviceIdType.MESH
BF = jnp.bfloat16
F32 = jnp.float32
HD = 128
T = 128
X = 4
Z = 8
NT = 8
KV = 8
GROUP = 4
NN = (((1,), (0,)), ((), ()))
NTD = (((1,), (1,)), ((), ()))
TN = (((0,), (0,)), ((), ()))
Z_STEPS = (4, 2, 6, 3, 5, 1, 7)
PLACE = {4: 0, 2: 1, 0: 2, 6: 3, 3: 4, 5: 5, 7: 6, 1: 7}


def dot(a, b, dims=NN):
    return lax.dot_general(a, b, dims, preferred_element_type=F32)


def tile(index, size=128):
    start = index * size
    if not isinstance(index, int):
        start = pl.multiple_of(start, size)
    return pl.ds(start, size)


def seat(c):
    return lax.rem(c, 2) * 4 + c // 2


def kernel(
    q_hbm, k_hbm, v_hbm, g_hbm, w_hbm, len_ref, grp_ref, off_ref,
    qg_hbm, kg_hbm, vg_hbm, wg_hbm,
    qg_ref, kg_ref, vg_ref, wg_ref,
    xin, wv, pack, mask, lab_s, lab_r,
    send, keep, got, gall,
    ag_s, ag_r, at_s, at_r, probs, outs, dk, dv,
    xs, xa, xr, zs, zr,
    in_sem, zsend, zrecv, qsend, qrecv, lsem, ysend, yrecv, csend, crecv,
    agsend, agrecv, atsend, atrecv, asend, arecv, xsend, xrecv, rsend, rrecv,
    out_sem,
):
    dp = lax.axis_index("dp")
    t = lax.axis_index("tensor")
    z = dp // X
    x = dp % X

    def at_z(d):
        return (lax.rem(z + d, Z) * X + x, t)

    def at_x(d):
        return (z * X + lax.rem(x + d, X), t)

    def at_t(d):
        return (dp, lax.rem(t + d, NT))

    partner = at_z(Z // 2)
    sibling_t = t + 1 - 2 * lax.rem(t, 2)
    sibling = (dp, sibling_t)

    def rcopy(src, dst, ssem, rsem, device):
        return pltpu.make_async_remote_copy(
            src_ref=src, dst_ref=dst, send_sem=ssem, recv_sem=rsem,
            device_id=device, device_id_type=MESH,
        )

    barrier = pltpu.get_barrier_semaphore()
    peers = [at_z(d) for d in range(1, Z)] + [at_x(d) for d in range(1, X)]
    peers = peers + [at_t(d) for d in range(1, NT)]
    for peer in peers:
        pl.semaphore_signal(barrier, inc=1, device_id=peer, device_id_type=MESH)

    loads = []
    for part in range(2):
        lanes = slice(part * 1024, 1024 + part * 3072)
        for slot in range(2):
            loads.append(
                pltpu.make_async_copy(
                    g_hbm.at[slot, :, lanes], xin.at[slot * T : (slot + 1) * T, lanes], in_sem.at[len(loads)]
                )
            )
    for hbm, start, width in ((k_hbm, 4096, 1024), (v_hbm, 5120, 1024), (q_hbm, 6144, 4096)):
        for slot in range(2):
            loads.append(
                pltpu.make_async_copy(
                    hbm.at[slot],
                    xin.at[slot * T : (slot + 1) * T, start : start + width],
                    in_sem.at[len(loads)],
                )
            )
    loads.append(pltpu.make_async_copy(w_hbm, wv, in_sem.at[len(loads)]))
    for load in loads:
        load.start()

    rows = lax.broadcasted_iota(jnp.int32, (T, T), 0)
    cols = lax.broadcasted_iota(jnp.int32, (T, T), 1)
    moved_off = jnp.int32(0)
    kept_off = jnp.int32(0)
    for slot in range(2):
        length = len_ref[slot]
        offset = off_ref[slot]
        moving = jnp.where(grp_ref[slot] != dp, 1, 0)
        hit = jnp.where((cols < length) & (rows == cols + offset), 1.0, 0.0)
        went = moving.astype(F32)
        pack[0:T, slot * T : (slot + 1) * T] = (hit * went).astype(BF)
        pack[T : 2 * T, slot * T : (slot + 1) * T] = (hit * (1.0 - went)).astype(BF)
        moved_off = moved_off + moving * offset
        kept_off = kept_off + (1 - moving) * offset
    lab_s[...] = jnp.zeros((8, 128), jnp.int32) + moved_off

    def zcopy(i):
        return rcopy(send.at[i], got.at[i], zsend.at[i], zrecv.at[i], partner)

    def qcopy(j, p):
        lanes = slice(p * 512, (p + 1) * 512)
        return rcopy(
            send.at[6 + j, :, lanes], got.at[6 + j, :, lanes], qsend.at[j, p], qrecv.at[j, p], partner
        )

    def start_q(j):
        for p in range(2):
            qcopy(j, p).start()

    label_copy = rcopy(lab_s, lab_r, lsem.at[0], lsem.at[1], partner)

    def packed(start):
        return dot(pack[...], xin[:, pl.ds(pl.multiple_of(start, 512), 512)])

    loads[0].wait()
    loads[1].wait()
    own_rows = tile(t)
    for i in range(4):
        for half in range(2):
            both = packed(i * 1024 + half * 512).astype(BF)
            send[i, :, half * 512 : (half + 1) * 512] = both[0:T]
            gall[own_rows, i * 1024 + half * 512 : i * 1024 + (half + 1) * 512] = both[T:]
        if i == 0:
            pl.semaphore_wait(barrier, len(peers))
            label_copy.start()
            zcopy(0).start()
            loads[2].wait()
            loads[3].wait()
        if i == 1:
            zcopy(1).start()
    for load in loads[4:10]:
        load.wait()
    for i in range(2):
        for half in range(2):
            both = packed(4096 + i * 1024 + half * 512).astype(BF)
            send[4 + i, :, half * 512 : (half + 1) * 512] = both[0:T]
            keep[i, :, half * 512 : (half + 1) * 512] = both[T:]

    def pack_q(c, carry):
        both = packed(6144 + c * 512).astype(BF)
        for j in range(GROUP):
            part = both[:, j * HD : (j + 1) * HD]
            send[6 + j, :, tile(seat(c))] = part[0:T]
            keep[2 + j, :, tile(seat(c))] = part[T:]
        return carry

    lax.fori_loop(0, KV, pack_q, 0)

    def block(i, row_t):
        return gall.at[tile(row_t), i * 1024 : (i + 1) * 1024]

    def ycopy(i, n, row_t):
        return rcopy(block(i, row_t), block(i, row_t), ysend.at[i, n], yrecv.at[i, n], at_t(2 * (n + 1)))

    def ccopy(i, n, row_t):
        return rcopy(block(i, row_t), block(i, row_t), csend.at[i, n], crecv.at[i, n], sibling)

    def from_t(n):
        return lax.rem(t + NT - 2 * (n + 1), NT)

    def sib_from_t(n):
        return lax.rem(sibling_t + NT - 2 * (n + 1), NT)

    def forward(i):
        for n in (0, 2, 1):
            ycopy(i, n, from_t(n)).wait_recv()
            ccopy(i, n, from_t(n)).start()

    for i in range(4):
        zcopy(i).wait_recv()
        zcopy(i + 2).start()
        lanes = slice(i * 1024, (i + 1) * 1024)
        gall[own_rows, lanes] = gall[own_rows, lanes] + got[i]
        for n in (1, 0, 2):
            ycopy(i, n, t).start()
        ccopy(i, 3, t).start()
        if i > 0:
            forward(i - 1)
    forward(3)
    loads[10].wait()
    for i in range(4):
        for n in range(3):
            ccopy(i, n, sib_from_t(n)).wait_recv()
        ccopy(i, 3, sibling_t).wait_recv()

    zcopy(4).wait_recv()
    start_q(0)

    def ag_copy(d):
        peer = lax.rem(t + d, NT)
        return rcopy(
            ag_s.at[tile(peer), :], ag_r.at[:, tile(t, 512)],
            agsend.at[d - 1], agrecv.at[d - 1], at_t(d),
        )

    def ag_got(d):
        source = lax.rem(t + NT - d, NT)
        return rcopy(
            ag_s.at[tile(source), :], ag_r.at[:, tile(source, 512)],
            agsend.at[d - 1], agrecv.at[d - 1], at_t(d),
        )

    def ag_block(peer):
        return dot(gall[tile(peer), :], wv[...], NTD).astype(BF)

    def ag_step(d, carry):
        peer = lax.rem(t + d, NT)
        ag_s[tile(peer), :] = ag_block(peer)
        ag_copy(d).start()
        return carry

    lax.fori_loop(1, NT, ag_step, 0)
    ag_r[:, tile(t, 512)] = ag_block(t)

    zcopy(5).wait_recv()
    start_q(1)
    label_copy.wait_recv()
    for i in range(2):
        keep[i] = keep[i] + got[4 + i]
    border = lab_r[0:1, :] + kept_off
    crossing = (rows >= border) & (cols < border)
    mask[...] = jnp.where((cols <= rows) & jnp.logical_not(crossing), 1.0, 0.0)
    dk[...] = jnp.zeros_like(dk)
    dv[...] = jnp.zeros_like(dv)
    scale = float(HD) ** (-0.5)
    last = GROUP - 1

    def at_copy(j, d):
        peer = lax.rem(t + d, NT)
        return rcopy(
            at_s.at[j, peer], at_r.at[j, t],
            atsend.at[j, d - 1], atrecv.at[j, d - 1], at_t(d),
        )

    def at_got(j, d):
        source = lax.rem(t + NT - d, NT)
        return rcopy(
            at_s.at[j, source], at_r.at[j, source],
            atsend.at[j, d - 1], atrecv.at[j, d - 1], at_t(d),
        )

    def distance(half, k):
        return lax.rem(4 + 6 * k, Z) if half == 0 else lax.rem(3 + 2 * k, Z)

    def rows_of(r):
        return slice(r * 64, (r + 1) * 64)

    def lanes_of(half):
        return slice(half * 512, (half + 1) * 512)

    def beside(s):
        return lax.rem(x + 1 + 2 * s, X)

    def relay_copy(j, half, s):
        return rcopy(
            xs.at[j, lax.rem(x + 2, X), rows_of(s), lanes_of(half)], xa.at[j, s, :, lanes_of(half)],
            asend.at[j, half, s], arecv.at[j, half, s], at_x(1 + 2 * s),
        )

    def xcopy(j, half, s, r):
        return rcopy(
            xs.at[j, beside(s), rows_of(r), lanes_of(half)], xr.at[j, s, rows_of(r), lanes_of(half)],
            xsend.at[j, half, s, r], xrecv.at[j, half, s, r], at_x(1 + 2 * s),
        )

    def rcopy_z(j, d):
        return rcopy(
            zs.at[j, PLACE[d]], zr.at[j, d - 1],
            rsend.at[j, d - 1], rrecv.at[j, d - 1], at_z(d),
        )

    def send_attended(j, p):
        def step(m, carry):
            peer = 2 * m + p

            @pl.when(peer != t)
            def _():
                at_copy(j, lax.rem(peer + NT - t, NT)).start()

            return carry

        lax.fori_loop(0, 4, step, 0)

    def forward_heads(j, p):
        four = range(4)
        allowed = mask[...] > 0.5
        scores = [
            dot(keep[2 + j, :, tile(p * 4 + m)], keep[0, :, tile(2 * m + p)], NTD) * scale for m in four
        ]
        scores = [jnp.where(allowed, score, -1e30) for score in scores]
        tops = [jnp.max(score, axis=-1, keepdims=True) for score in scores]
        expos = [jnp.exp(scores[m] - tops[m]) for m in four]
        sums = [jnp.sum(expo, axis=-1, keepdims=True) for expo in expos]
        prob = [expos[m] / sums[m] for m in four]
        out = [dot(prob[m].astype(BF), keep[1, :, tile(2 * m + p)]).astype(BF) for m in four]
        for m in four:
            at_s[j, 2 * m + p] = out[m].T
        for m in four:
            probs[2 * m + p] = prob[m]
            outs[2 * m + p] = out[m]

    def backward_heads(j, p):
        def step(p, carry):
            four = range(4)
            heads = [2 * m + p for m in four]
            query = [keep[2 + j, :, tile(p * 4 + m)] for m in four]
            key = [keep[0, :, tile(c)] for c in heads]
            value = [keep[1, :, tile(c)] for c in heads]
            grad = [ag_r[:, tile(c * GROUP + j)] for c in heads]
            prob = [probs[c] for c in heads]
            delta = [
                jnp.sum(grad[m].astype(F32) * outs[heads[m]].astype(F32), axis=-1, keepdims=True) for m in four
            ]
            prob_grad = [dot(grad[m], value[m], NTD) for m in four]
            score_grad = [(prob[m] * (prob_grad[m] - delta[m])).astype(BF) for m in four]
            query_grad = [(dot(score_grad[m], key[m]) * scale).astype(BF) for m in four]
            key_grad = [dk[heads[m]] + dot(score_grad[m], query[m], TN) for m in four]
            value_grad = [dv[heads[m]] + dot(prob[m].astype(BF), grad[m], TN) for m in four]
            for m in four:
                qg_ref[:, tile(heads[m] * GROUP + j)] = query_grad[m]
                dk[heads[m]] = key_grad[m]
                dv[heads[m]] = value_grad[m]
            return carry

        lax.fori_loop(p, p + 1, step, 0)

    def relay_x(j, half):
        lanes = lanes_of(half)
        for s in range(2):
            relay_copy(j, half, s).wait_recv()
            mine = xs[j, beside(s), rows_of(s), lanes].astype(F32)
            xs[j, beside(s), rows_of(s), lanes] = (mine + xa[j, s, :, lanes].astype(F32)).astype(BF)
            xcopy(j, half, s, s).start()

    def reduce_x(j, half):
        for s in range(2):
            xcopy(j, half, s, 1 - s).wait_recv()
        for s in range(2):
            xcopy(j, half, s, s).wait_recv()

        def step(k, carry):
            place = half * 4 + k
            total = xs[j, x, :, tile(place)].astype(F32)
            for s in range(2):
                total = total + xr[j, s, :, tile(place)].astype(F32)
            zs[j, place] = total.astype(BF)
            return carry

        lax.fori_loop(0, 4, step, 0)

    def send_z(j, half):
        for d in ((4, 2, 6), (3, 5, 1, 7))[half]:
            rcopy_z(j, d).start()

    def reduce_z(j):
        total = zs[j, PLACE[0]].astype(F32)
        for d in Z_STEPS:
            rcopy_z(j, d).wait_recv()
            total = total + zr[j, d - 1].astype(F32)
        wg_ref[j * HD : (j + 1) * HD, :] = total

    def weight_term(j, half):
        def step(k, carry):
            place = half * 4 + k
            zz = lax.rem(z + distance(half, k), Z)
            attended = jnp.concatenate([at_r[j, source] for source in range(NT)], axis=1)
            term = dot(attended, gall[:, tile(zz, 512)]).astype(BF)
            for xx in range(X):
                xs[j, xx, :, tile(place)] = term[:, xx * HD : (xx + 1) * HD]
            return carry

        lax.fori_loop(0, 4, step, 0)
        for s in range(2):
            relay_copy(j, half, s).start()
        for s in range(2):
            xcopy(j, half, s, 1 - s).start()

    def weight_chunk(j):
        for d in range(1, NT):
            at_got(j, d).wait_recv()
        for half in range(2):
            weight_term(j, half)

    for j in range(GROUP):
        for p in range(2):
            qcopy(j, p).wait_recv()
            if p == 1 and j < 2:
                qcopy(j + 2, 0).start()
            lanes = slice(p * 512, (p + 1) * 512)
            keep[2 + j, :, lanes] = keep[2 + j, :, lanes] + got[6 + j, :, lanes]
            forward_heads(j, p)
            send_attended(j, p)
            if p == 0:
                if j == 0:
                    for d in range(1, NT):
                        ag_got(d).wait_recv()
                backward_heads(j, 0)
        at_r[j, t] = at_s[j, t]
        if j == last:
            for i in range(last - 1):
                send_z(i, 0)
                send_z(i, 1)
        if j > 0:
            for half in range(2):
                relay_x(j - 1, half)
        if j < last:
            backward_heads(j, 1)
        if j < 2:
            qcopy(j + 2, 1).start()
        weight_chunk(j)
        if j > 0 and j < last:
            for half in range(2):
                reduce_x(j - 1, half)
    for half in range(2):
        reduce_x(last - 1, half)
        send_z(last - 1, half)
    for half in range(2):
        relay_x(last, half)
    backward_heads(last, 1)
    for c in range(KV):
        kg_ref[:, c * HD : (c + 1) * HD] = (dk[c] * scale).astype(BF)
        vg_ref[:, c * HD : (c + 1) * HD] = dv[c].astype(BF)
    stores = [
        pltpu.make_async_copy(held, out, out_sem.at[i])
        for i, (held, out) in enumerate(((qg_ref, qg_hbm), (kg_ref, kg_hbm), (vg_ref, vg_hbm), (wg_ref, wg_hbm)))
    ]
    for store in stores[:3]:
        store.start()
    for half in range(2):
        reduce_x(last, half)
        send_z(last, half)
    for j in range(last):
        reduce_z(j)

    label_copy.wait_send()
    for i in range(6):
        zcopy(i).wait_send()
    for j in range(GROUP):
        for p in range(2):
            qcopy(j, p).wait_send()
    for i in range(4):
        for n in range(3):
            ycopy(i, n, t).wait_send()
            ccopy(i, n, from_t(n)).wait_send()
        ccopy(i, 3, t).wait_send()
    for d in range(1, NT):
        ag_copy(d).wait_send()
    for j in range(GROUP):
        for d in range(1, NT):
            at_copy(j, d).wait_send()
        for half in range(2):
            for s in range(2):
                relay_copy(j, half, s).wait_send()
                for r in range(2):
                    xcopy(j, half, s, r).wait_send()
    reduce_z(GROUP - 1)
    stores[3].start()
    for j in range(GROUP):
        for d in Z_STEPS:
            rcopy_z(j, d).wait_send()
    for store in stores:
        store.wait()


def deliver(*refs):
    sources, targets, held = refs[:4], refs[4:8], refs[8:12]
    load_sem, store_sem = refs[12:]
    pieces = []
    for n in range(4):
        size = sources[n].shape[0] // 4
        for part in range(4 if n == 0 else 1):
            rows = slice(part * size, (part + 1) * size) if n == 0 else slice(0, size * 4)
            at = len(pieces)
            pieces.append((
                pltpu.make_async_copy(sources[n].at[rows], held[n].at[rows], load_sem.at[at]),
                pltpu.make_async_copy(held[n].at[rows], targets[n].at[rows], store_sem.at[at]),
            ))
    for load, _ in pieces:
        load.start()
    for load, store in pieces:
        load.wait()
        store.start()
    for _, store in pieces:
        store.wait()


def local(queries, keys, values, out_grad, out_weight, lengths, dest_group, dest_offset):
    dma = pltpu.SemaphoreType.DMA
    vm = pltpu.VMEM
    results = pl.pallas_call(
        kernel,
        out_shape=(
            jax.ShapeDtypeStruct((T, 4096), BF),
            jax.ShapeDtypeStruct((T, 1024), BF),
            jax.ShapeDtypeStruct((T, 1024), BF),
            jax.ShapeDtypeStruct((512, 128), F32),
        ),
        in_specs=[pl.BlockSpec(memory_space=pl.ANY)] * 5 + [pl.BlockSpec(memory_space=pltpu.SMEM)] * 3,
        out_specs=tuple([pl.BlockSpec(memory_space=pl.ANY)] * 4),
        scratch_shapes=[
            vm((T, 4096), BF),
            vm((T, 1024), BF),
            vm((T, 1024), BF),
            vm((512, 128), F32),
            vm((2 * T, 10240), BF),
            vm((512, 4096), BF),
            vm((2 * T, 2 * T), BF),
            vm((T, T), F32),
            vm((8, 128), jnp.int32),
            vm((8, 128), jnp.int32),
            vm((10, T, 1024), BF),
            vm((6, T, 1024), BF),
            vm((10, T, 1024), BF),
            vm((NT * T, 4096), BF),
            vm((NT * T, 512), BF),
            vm((T, 4096), BF),
            vm((GROUP, KV, HD, T), BF),
            vm((GROUP, NT, HD, T), BF),
            vm((KV, T, T), F32),
            vm((KV, T, HD), BF),
            vm((KV, T, HD), F32),
            vm((KV, T, HD), F32),
            vm((GROUP, X, HD, 1024), BF),
            vm((GROUP, 2, HD // 2, 1024), BF),
            vm((GROUP, 2, HD, 1024), BF),
            vm((GROUP, Z, HD, 128), BF),
            vm((GROUP, Z - 1, HD, 128), BF),
            dma((11,)),
            dma((6,)), dma((6,)),
            dma((4, 2)), dma((4, 2)),
            dma((2,)),
            dma((4, 3)), dma((4, 3)),
            dma((4, 4)), dma((4, 4)),
            dma((7,)), dma((7,)),
            dma((4, 7)), dma((4, 7)),
            dma((4, 2, 2)), dma((4, 2, 2)),
            dma((4, 2, 2, 2)), dma((4, 2, 2, 2)),
            dma((4, 7)), dma((4, 7)),
            dma((4,)),
        ],
        compiler_params=pltpu.CompilerParams(
            collective_id=0, has_side_effects=True, vmem_limit_bytes=60 * 2**20
        ),
        cost_estimate=pl.CostEstimate(flops=30_000_000_000, bytes_accessed=12_000_000, transcendentals=600_000),
    )(queries, keys, values, out_grad, out_weight, lengths, dest_group, dest_offset)
    return pl.pallas_call(
        deliver,
        out_shape=tuple(jax.ShapeDtypeStruct(r.shape, r.dtype) for r in results),
        in_specs=[pl.BlockSpec(memory_space=pl.ANY)] * 4,
        out_specs=tuple([pl.BlockSpec(memory_space=pl.ANY)] * 4),
        scratch_shapes=[vm(r.shape, r.dtype) for r in results] + [dma((7,)), dma((7,))],
    )(*results)


def solution(mesh):
    in_specs = (
        P(("dp", "tensor"), None, None),
        P(("dp", "tensor"), None, None),
        P(("dp", "tensor"), None, None),
        P(("dp", "tensor"), None, None),
        P("tensor", None),
        P(("dp", "tensor")),
        P(("dp", "tensor")),
        P(("dp", "tensor")),
    )
    out_specs = (
        P(("dp", "tensor"), None),
        P(("dp", "tensor"), None),
        P(("dp", "tensor"), None),
        P("tensor", "dp"),
    )
    return jax.shard_map(local, mesh=mesh, in_specs=in_specs, out_specs=out_specs, check_vma=False)
```

```python
import functools

import jax
import jax.numpy as jnp
from jax import lax
from jax.experimental import pallas as pl
from jax.experimental.pallas import tpu as pltpu
from jax.sharding import PartitionSpec as P

MESH = pl.DeviceIdType.MESH
BF = jnp.bfloat16
F32 = jnp.float32
HD = 128
T = 128
X = 4
Z = 8
NT = 8
KV = 8
GROUP = 4
NN = (((1,), (0,)), ((), ()))
NTD = (((1,), (1,)), ((), ()))
TN = (((0,), (0,)), ((), ()))
Z_STEPS = (4, 2, 6, 3, 5, 1, 7)
PLACE = {4: 0, 2: 1, 0: 2, 6: 3, 3: 4, 5: 5, 7: 6, 1: 7}


def dot(a, b, dims=NN):
    return lax.dot_general(a, b, dims, preferred_element_type=F32)


def tile(index, size=128):
    start = index * size
    if not isinstance(index, int):
        start = pl.multiple_of(start, size)
    return pl.ds(start, size)


def seat(c):
    return lax.rem(c, 2) * 4 + c // 2


def kernel(
    q_hbm, k_hbm, v_hbm, g_hbm, w_hbm, len_ref, grp_ref, off_ref,
    qg_hbm, kg_hbm, vg_hbm, wg_hbm,
    qg_ref, kg_ref, vg_ref, wg_ref,
    xin, wv, pack, mask, lab_s, lab_r,
    send, keep, got, gall,
    ag_s, ag_r, at_s, at_r, probs, outs, dk, dv,
    xs, xa, xr, zs, zr,
    in_sem, zsend, zrecv, qsend, qrecv, lsem, ysend, yrecv, csend, crecv,
    agsend, agrecv, atsend, atrecv, asend, arecv, xsend, xrecv, rsend, rrecv,
    out_sem,
):
    dp = lax.axis_index("dp")
    t = lax.axis_index("tensor")
    z = dp // X
    x = dp % X

    def at_z(d):
        return (lax.rem(z + d, Z) * X + x, t)

    def at_x(d):
        return (z * X + lax.rem(x + d, X), t)

    def at_t(d):
        return (dp, lax.rem(t + d, NT))

    partner = at_z(Z // 2)
    sibling_t = t + 1 - 2 * lax.rem(t, 2)
    sibling = (dp, sibling_t)

    def rcopy(src, dst, ssem, rsem, device):
        return pltpu.make_async_remote_copy(
            src_ref=src, dst_ref=dst, send_sem=ssem, recv_sem=rsem,
            device_id=device, device_id_type=MESH,
        )

    barrier = pltpu.get_barrier_semaphore()
    peers = [at_z(d) for d in range(1, Z)] + [at_x(d) for d in range(1, X)]
    peers = peers + [at_t(d) for d in range(1, NT)]
    loads = []
    for part in range(2):
        lanes = slice(part * 1024, 1024 + part * 3072)
        for slot in range(2):
            loads.append(
                pltpu.make_async_copy(
                    g_hbm.at[slot, :, lanes], xin.at[slot * T : (slot + 1) * T, lanes], in_sem.at[len(loads)]
                )
            )
    for hbm, start, width in ((k_hbm, 4096, 1024), (v_hbm, 5120, 1024), (q_hbm, 6144, 4096)):
        for slot in range(2):
            loads.append(
                pltpu.make_async_copy(
                    hbm.at[slot],
                    xin.at[slot * T : (slot + 1) * T, start : start + width],
                    in_sem.at[len(loads)],
                )
            )
    loads.append(pltpu.make_async_copy(w_hbm, wv, in_sem.at[len(loads)]))
    for load in loads[:2]:
        load.start()
    for peer in peers:
        pl.semaphore_signal(barrier, inc=1, device_id=peer, device_id_type=MESH)

    for load in loads[2:]:
        load.start()

    rows = lax.broadcasted_iota(jnp.int32, (T, T), 0)
    cols = lax.broadcasted_iota(jnp.int32, (T, T), 1)
    moved_off = jnp.int32(0)
    kept_off = jnp.int32(0)
    for slot in range(2):
        length = len_ref[slot]
        offset = off_ref[slot]
        moving = jnp.where(grp_ref[slot] != dp, 1, 0)
        hit = jnp.where((cols < length) & (rows == cols + offset), 1.0, 0.0)
        went = moving.astype(F32)
        pack[0:T, slot * T : (slot + 1) * T] = (hit * went).astype(BF)
        pack[T : 2 * T, slot * T : (slot + 1) * T] = (hit * (1.0 - went)).astype(BF)
        moved_off = moved_off + moving * offset
        kept_off = kept_off + (1 - moving) * offset
    lab_s[...] = jnp.zeros((8, 128), jnp.int32) + moved_off

    def zcopy(i):
        return rcopy(send.at[i], got.at[i], zsend.at[i], zrecv.at[i], partner)

    def qcopy(j, p):
        lanes = slice(p * 512, (p + 1) * 512)
        return rcopy(
            send.at[6 + j, :, lanes], got.at[6 + j, :, lanes], qsend.at[j, p], qrecv.at[j, p], partner
        )

    def start_q(j):
        for p in range(2):
            qcopy(j, p).start()

    label_copy = rcopy(lab_s, lab_r, lsem.at[0], lsem.at[1], partner)

    def packed(start):
        return dot(pack[...], xin[:, pl.ds(pl.multiple_of(start, 512), 512)])

    loads[0].wait()
    loads[1].wait()
    own_rows = tile(t)
    for i in range(4):
        for half in range(2):
            both = packed(i * 1024 + half * 512).astype(BF)
            send[i, :, half * 512 : (half + 1) * 512] = both[0:T]
            gall[own_rows, i * 1024 + half * 512 : i * 1024 + (half + 1) * 512] = both[T:]
        if i == 0:
            pl.semaphore_wait(barrier, len(peers))
            label_copy.start()
            zcopy(0).start()
            loads[2].wait()
            loads[3].wait()
        if i == 1:
            zcopy(1).start()
    for load in loads[4:10]:
        load.wait()
    for i in range(2):
        for half in range(2):
            both = packed(4096 + i * 1024 + half * 512).astype(BF)
            send[4 + i, :, half * 512 : (half + 1) * 512] = both[0:T]
            keep[i, :, half * 512 : (half + 1) * 512] = both[T:]

    def pack_q(c, carry):
        both = packed(6144 + c * 512).astype(BF)
        for j in range(GROUP):
            part = both[:, j * HD : (j + 1) * HD]
            send[6 + j, :, tile(seat(c))] = part[0:T]
            keep[2 + j, :, tile(seat(c))] = part[T:]
        return carry

    lax.fori_loop(0, KV, pack_q, 0)

    def block(i, row_t):
        return gall.at[tile(row_t), i * 1024 : (i + 1) * 1024]

    def ycopy(i, n, row_t):
        return rcopy(block(i, row_t), block(i, row_t), ysend.at[i, n], yrecv.at[i, n], at_t(2 * (n + 1)))

    def ccopy(i, n, row_t):
        return rcopy(block(i, row_t), block(i, row_t), csend.at[i, n], crecv.at[i, n], sibling)

    def from_t(n):
        return lax.rem(t + NT - 2 * (n + 1), NT)

    def sib_from_t(n):
        return lax.rem(sibling_t + NT - 2 * (n + 1), NT)

    def forward(i):
        for n in (0, 2, 1):
            ycopy(i, n, from_t(n)).wait_recv()
            ccopy(i, n, from_t(n)).start()

    for i in range(4):
        zcopy(i).wait_recv()
        zcopy(i + 2).start()
        lanes = slice(i * 1024, (i + 1) * 1024)
        gall[own_rows, lanes] = gall[own_rows, lanes] + got[i]
        for n in (1, 0, 2):
            ycopy(i, n, t).start()
        ccopy(i, 3, t).start()
        if i > 0:
            forward(i - 1)
    forward(3)
    loads[10].wait()
    for i in range(4):
        for n in range(3):
            ccopy(i, n, sib_from_t(n)).wait_recv()
        ccopy(i, 3, sibling_t).wait_recv()

    zcopy(4).wait_recv()
    start_q(0)

    def ag_copy(d):
        peer = lax.rem(t + d, NT)
        return rcopy(
            ag_s.at[tile(peer), :], ag_r.at[:, tile(t, 512)],
            agsend.at[d - 1], agrecv.at[d - 1], at_t(d),
        )

    def ag_got(d):
        source = lax.rem(t + NT - d, NT)
        return rcopy(
            ag_s.at[tile(source), :], ag_r.at[:, tile(source, 512)],
            agsend.at[d - 1], agrecv.at[d - 1], at_t(d),
        )

    def ag_block(peer):
        return dot(gall[tile(peer), :], wv[...], NTD).astype(BF)

    def ag_step(d, carry):
        peer = lax.rem(t + d, NT)
        ag_s[tile(peer), :] = ag_block(peer)
        ag_copy(d).start()
        return carry

    lax.fori_loop(1, NT, ag_step, 0)
    ag_r[:, tile(t, 512)] = ag_block(t)

    zcopy(5).wait_recv()
    start_q(1)
    label_copy.wait_recv()
    for i in range(2):
        keep[i] = keep[i] + got[4 + i]
    border = lab_r[0:1, :] + kept_off
    crossing = (rows >= border) & (cols < border)
    mask[...] = jnp.where((cols <= rows) & jnp.logical_not(crossing), 1.0, 0.0)
    dk[...] = jnp.zeros_like(dk)
    dv[...] = jnp.zeros_like(dv)
    scale = float(HD) ** (-0.5)
    last = GROUP - 1

    def at_copy(j, d):
        peer = lax.rem(t + d, NT)
        return rcopy(
            at_s.at[j, peer], at_r.at[j, t],
            atsend.at[j, d - 1], atrecv.at[j, d - 1], at_t(d),
        )

    def at_got(j, d):
        source = lax.rem(t + NT - d, NT)
        return rcopy(
            at_s.at[j, source], at_r.at[j, source],
            atsend.at[j, d - 1], atrecv.at[j, d - 1], at_t(d),
        )

    def distance(half, k):
        return lax.rem(4 + 6 * k, Z) if half == 0 else lax.rem(3 + 2 * k, Z)

    def rows_of(r):
        return slice(r * 64, (r + 1) * 64)

    def lanes_of(half):
        return slice(half * 512, (half + 1) * 512)

    def beside(s):
        return lax.rem(x + 1 + 2 * s, X)

    def relay_copy(j, half, s):
        return rcopy(
            xs.at[j, lax.rem(x + 2, X), rows_of(s), lanes_of(half)], xa.at[j, s, :, lanes_of(half)],
            asend.at[j, half, s], arecv.at[j, half, s], at_x(1 + 2 * s),
        )

    def xcopy(j, half, s, r):
        return rcopy(
            xs.at[j, beside(s), rows_of(r), lanes_of(half)], xr.at[j, s, rows_of(r), lanes_of(half)],
            xsend.at[j, half, s, r], xrecv.at[j, half, s, r], at_x(1 + 2 * s),
        )

    def rcopy_z(j, d):
        return rcopy(
            zs.at[j, PLACE[d]], zr.at[j, d - 1],
            rsend.at[j, d - 1], rrecv.at[j, d - 1], at_z(d),
        )

    def send_attended(j, p):
        def step(m, carry):
            peer = 2 * m + p

            @pl.when(peer != t)
            def _():
                at_copy(j, lax.rem(peer + NT - t, NT)).start()

            return carry

        lax.fori_loop(0, 4, step, 0)

    def forward_heads(j, p):
        four = range(4)
        allowed = mask[...] > 0.5
        scores = [
            dot(keep[2 + j, :, tile(p * 4 + m)], keep[0, :, tile(2 * m + p)], NTD) * scale for m in four
        ]
        scores = [jnp.where(allowed, score, -1e30) for score in scores]
        tops = [jnp.max(score, axis=-1, keepdims=True) for score in scores]
        expos = [jnp.exp(scores[m] - tops[m]) for m in four]
        sums = [jnp.sum(expo, axis=-1, keepdims=True) for expo in expos]
        prob = [expos[m] / sums[m] for m in four]
        out = [dot(prob[m].astype(BF), keep[1, :, tile(2 * m + p)]).astype(BF) for m in four]
        for m in four:
            at_s[j, 2 * m + p] = out[m].T
        for m in four:
            probs[2 * m + p] = prob[m]
            outs[2 * m + p] = out[m]

    def backward_heads(j, p):
        def step(p, carry):
            four = range(4)
            heads = [2 * m + p for m in four]
            query = [keep[2 + j, :, tile(p * 4 + m)] for m in four]
            key = [keep[0, :, tile(c)] for c in heads]
            value = [keep[1, :, tile(c)] for c in heads]
            grad = [ag_r[:, tile(c * GROUP + j)] for c in heads]
            prob = [probs[c] for c in heads]
            delta = [
                jnp.sum(grad[m].astype(F32) * outs[heads[m]].astype(F32), axis=-1, keepdims=True) for m in four
            ]
            prob_grad = [dot(grad[m], value[m], NTD) for m in four]
            score_grad = [(prob[m] * (prob_grad[m] - delta[m])).astype(BF) for m in four]
            query_grad = [(dot(score_grad[m], key[m]) * scale).astype(BF) for m in four]
            key_grad = [dk[heads[m]] + dot(score_grad[m], query[m], TN) for m in four]
            value_grad = [dv[heads[m]] + dot(prob[m].astype(BF), grad[m], TN) for m in four]
            for m in four:
                qg_ref[:, tile(heads[m] * GROUP + j)] = query_grad[m]
                dk[heads[m]] = key_grad[m]
                dv[heads[m]] = value_grad[m]
            return carry

        lax.fori_loop(p, p + 1, step, 0)

    def relay_x(j, half):
        lanes = lanes_of(half)
        for s in range(2):
            relay_copy(j, half, s).wait_recv()
            mine = xs[j, beside(s), rows_of(s), lanes].astype(F32)
            xs[j, beside(s), rows_of(s), lanes] = (mine + xa[j, s, :, lanes].astype(F32)).astype(BF)
            xcopy(j, half, s, s).start()

    def reduce_x(j, half):
        for s in range(2):
            xcopy(j, half, s, 1 - s).wait_recv()
        for s in range(2):
            xcopy(j, half, s, s).wait_recv()

        def step(k, carry):
            place = half * 4 + k
            total = xs[j, x, :, tile(place)].astype(F32)
            for s in range(2):
                total = total + xr[j, s, :, tile(place)].astype(F32)
            zs[j, place] = total.astype(BF)
            return carry

        lax.fori_loop(0, 4, step, 0)

    def send_z(j, half):
        for d in ((4, 2, 6), (3, 5, 1, 7))[half]:
            rcopy_z(j, d).start()

    def reduce_z(j):
        total = zs[j, PLACE[0]].astype(F32)
        for d in Z_STEPS:
            rcopy_z(j, d).wait_recv()
            total = total + zr[j, d - 1].astype(F32)
        wg_ref[j * HD : (j + 1) * HD, :] = total

    def weight_term(j, half):
        def step(k, carry):
            place = half * 4 + k
            zz = lax.rem(z + distance(half, k), Z)
            attended = jnp.concatenate([at_r[j, source] for source in range(NT)], axis=1)
            term = dot(attended, gall[:, tile(zz, 512)]).astype(BF)
            for xx in range(X):
                xs[j, xx, :, tile(place)] = term[:, xx * HD : (xx + 1) * HD]
            return carry

        lax.fori_loop(0, 4, step, 0)
        for s in range(2):
            relay_copy(j, half, s).start()
        for s in range(2):
            xcopy(j, half, s, 1 - s).start()

    def weight_chunk(j):
        for d in range(1, NT):
            at_got(j, d).wait_recv()
        for half in range(2):
            weight_term(j, half)

    for j in range(GROUP):
        for p in range(2):
            qcopy(j, p).wait_recv()
            if p == 1 and j < 2:
                qcopy(j + 2, 0).start()
            lanes = slice(p * 512, (p + 1) * 512)
            keep[2 + j, :, lanes] = keep[2 + j, :, lanes] + got[6 + j, :, lanes]
            forward_heads(j, p)
            send_attended(j, p)
            if p == 0:
                if j == 0:
                    for d in range(1, NT):
                        ag_got(d).wait_recv()
                backward_heads(j, 0)
        at_r[j, t] = at_s[j, t]
        if j == last:
            for i in range(last - 1):
                send_z(i, 0)
                send_z(i, 1)
        if j > 0:
            for half in range(2):
                relay_x(j - 1, half)
        if j < last:
            backward_heads(j, 1)
        if j < 2:
            qcopy(j + 2, 1).start()
        weight_chunk(j)
        if j > 0 and j < last:
            for half in range(2):
                reduce_x(j - 1, half)
    for half in range(2):
        reduce_x(last - 1, half)
        send_z(last - 1, half)
    for half in range(2):
        relay_x(last, half)
    backward_heads(last, 1)
    for c in range(KV):
        kg_ref[:, c * HD : (c + 1) * HD] = (dk[c] * scale).astype(BF)
        vg_ref[:, c * HD : (c + 1) * HD] = dv[c].astype(BF)
    stores = [
        pltpu.make_async_copy(held, out, out_sem.at[i])
        for i, (held, out) in enumerate((
            (qg_ref, qg_hbm), (kg_ref, kg_hbm), (vg_ref, vg_hbm),
            (wg_ref.at[0:384], wg_hbm.at[0:384]), (wg_ref.at[384:512], wg_hbm.at[384:512]),
        ))
    ]
    for store in stores[:3]:
        store.start()
    for half in range(2):
        reduce_x(last, half)
        send_z(last, half)
    for j in range(last):
        reduce_z(j)
    stores[3].start()

    label_copy.wait_send()
    for i in range(6):
        zcopy(i).wait_send()
    for j in range(GROUP):
        for p in range(2):
            qcopy(j, p).wait_send()
    for i in range(4):
        for n in range(3):
            ycopy(i, n, t).wait_send()
            ccopy(i, n, from_t(n)).wait_send()
        ccopy(i, 3, t).wait_send()
    for d in range(1, NT):
        ag_copy(d).wait_send()
    for j in range(GROUP):
        for d in range(1, NT):
            at_copy(j, d).wait_send()
        for half in range(2):
            for s in range(2):
                relay_copy(j, half, s).wait_send()
                for r in range(2):
                    xcopy(j, half, s, r).wait_send()
    reduce_z(GROUP - 1)
    stores[4].start()
    for j in range(GROUP):
        for d in Z_STEPS:
            rcopy_z(j, d).wait_send()
    for store in stores:
        store.wait()


def deliver(*refs):
    sources, targets, held = refs[:4], refs[4:8], refs[8:12]
    load_sem, store_sem = refs[12:]
    pieces = []
    for n in range(4):
        size = sources[n].shape[0] // 4
        for part in range(4 if n == 0 else 1):
            rows = slice(part * size, (part + 1) * size) if n == 0 else slice(0, size * 4)
            at = len(pieces)
            pieces.append((
                pltpu.make_async_copy(sources[n].at[rows], held[n].at[rows], load_sem.at[at]),
                pltpu.make_async_copy(held[n].at[rows], targets[n].at[rows], store_sem.at[at]),
            ))
    for load, _ in pieces:
        load.start()
    for load, store in pieces:
        load.wait()
        store.start()
    for _, store in pieces:
        store.wait()


def local(queries, keys, values, out_grad, out_weight, lengths, dest_group, dest_offset):
    dma = pltpu.SemaphoreType.DMA
    vm = pltpu.VMEM
    results = pl.pallas_call(
        kernel,
        out_shape=(
            jax.ShapeDtypeStruct((T, 4096), BF),
            jax.ShapeDtypeStruct((T, 1024), BF),
            jax.ShapeDtypeStruct((T, 1024), BF),
            jax.ShapeDtypeStruct((512, 128), F32),
        ),
        in_specs=[pl.BlockSpec(memory_space=pl.ANY)] * 5 + [pl.BlockSpec(memory_space=pltpu.SMEM)] * 3,
        out_specs=tuple([pl.BlockSpec(memory_space=pl.ANY)] * 4),
        scratch_shapes=[
            vm((T, 4096), BF),
            vm((T, 1024), BF),
            vm((T, 1024), BF),
            vm((512, 128), F32),
            vm((2 * T, 10240), BF),
            vm((512, 4096), BF),
            vm((2 * T, 2 * T), BF),
            vm((T, T), F32),
            vm((8, 128), jnp.int32),
            vm((8, 128), jnp.int32),
            vm((10, T, 1024), BF),
            vm((6, T, 1024), BF),
            vm((10, T, 1024), BF),
            vm((NT * T, 4096), BF),
            vm((NT * T, 512), BF),
            vm((T, 4096), BF),
            vm((GROUP, KV, HD, T), BF),
            vm((GROUP, NT, HD, T), BF),
            vm((KV, T, T), F32),
            vm((KV, T, HD), BF),
            vm((KV, T, HD), F32),
            vm((KV, T, HD), F32),
            vm((GROUP, X, HD, 1024), BF),
            vm((GROUP, 2, HD // 2, 1024), BF),
            vm((GROUP, 2, HD, 1024), BF),
            vm((GROUP, Z, HD, 128), BF),
            vm((GROUP, Z - 1, HD, 128), BF),
            dma((11,)),
            dma((6,)), dma((6,)),
            dma((4, 2)), dma((4, 2)),
            dma((2,)),
            dma((4, 3)), dma((4, 3)),
            dma((4, 4)), dma((4, 4)),
            dma((7,)), dma((7,)),
            dma((4, 7)), dma((4, 7)),
            dma((4, 2, 2)), dma((4, 2, 2)),
            dma((4, 2, 2, 2)), dma((4, 2, 2, 2)),
            dma((4, 7)), dma((4, 7)),
            dma((5,)),
        ],
        compiler_params=pltpu.CompilerParams(
            collective_id=0, has_side_effects=True, vmem_limit_bytes=60 * 2**20
        ),
        cost_estimate=pl.CostEstimate(flops=30_000_000_000, bytes_accessed=12_000_000, transcendentals=600_000),
    )(queries, keys, values, out_grad, out_weight, lengths, dest_group, dest_offset)
    return pl.pallas_call(
        deliver,
        out_shape=tuple(jax.ShapeDtypeStruct(r.shape, r.dtype) for r in results),
        in_specs=[pl.BlockSpec(memory_space=pl.ANY)] * 4,
        out_specs=tuple([pl.BlockSpec(memory_space=pl.ANY)] * 4),
        scratch_shapes=[vm(r.shape, r.dtype) for r in results] + [dma((7,)), dma((7,))],
    )(*results)


def solution(mesh):
    in_specs = (
        P(("dp", "tensor"), None, None),
        P(("dp", "tensor"), None, None),
        P(("dp", "tensor"), None, None),
        P(("dp", "tensor"), None, None),
        P("tensor", None),
        P(("dp", "tensor")),
        P(("dp", "tensor")),
        P(("dp", "tensor")),
    )
    out_specs = (
        P(("dp", "tensor"), None),
        P(("dp", "tensor"), None),
        P(("dp", "tensor"), None),
        P("tensor", "dp"),
    )
    return jax.shard_map(local, mesh=mesh, in_specs=in_specs, out_specs=out_specs, check_vma=False)
```
